512 devices in a mesh: range: 128 (over y, z, core), dp: 4 (over x).
Axes of the slice: x: 4, y: 8, z: 8, core: 2. Of those that a mesh axis runs over, the one named last changes fastest.
Arguments:
- node_feats: bfloat16 [4, 32768, 256], P('dp', 'range'), may hold values from -6 to 6
- ctx_table: bfloat16 [4, 16384, 256], P('dp', 'range'), may hold values from -6 to 6
- fetch_rows: int32 [4, 128, 128, 8], P('dp', 'range'), may hold values from 0 to 127
- ctx_slot: int32 [4, 32768, 4], P('dp', 'range'), may hold values from 0 to 1023, as said below
- labels: int32 [4, 32768], P('dp', 'range'), may hold values from 1 to 255
- relay_slot: int32 [4, 32768], P('dp', 'range'), may hold values from 0 to 255, as said below
- w_ctx: bfloat16 [1024, 256], replicated, may hold values from -0.1875 to 0.1875
- w_query: bfloat16 [256, 256], replicated, may hold values from -8 to 8
- w_key: bfloat16 [256, 256], replicated, may hold values from -8 to 8
- w_value: bfloat16 [256, 256], replicated, may hold values from -0.375 to 0.375
- w_proj: bfloat16 [256, 256], replicated, may hold values from -0.375 to 0.375
- w_logit: bfloat16 [256, 256], replicated, may hold values from -1.2 to 1.2
- gain_attn: float32 [256], replicated, may hold values from 0.4 to 1.6
- gain_out: float32 [256], replicated, may hold values from 0.4 to 1.6
Outputs:
- relayed: bfloat16 [4, 32768, 256], P('dp', 'range')
- loss_total: float32 [], replicated
- grad_ctx: float32 [1024, 256], replicated
- grad_query: float32 [256, 256], replicated
- grad_key: float32 [256, 256], replicated
- grad_value: float32 [256, 256], replicated
- grad_proj: float32 [256, 256], replicated
- grad_logit: float32 [256, 256], replicated
- grad_gain_attn: float32 [256], replicated
- grad_gain_out: float32 [256], replicated
The draws below stay inside these ranges and needn't reach their ends.
Inputs may be any that keep to these rules, and one draw needn't show every extreme that they name: `ctx_slot`: within each window the 1024 entries name every one of the 1024 fetched rows equally often. `relay_slot`: within each window a permutation of the offsets; offset s belongs to owner s // 2 of the tile.
All inputs are finite; a program needn't handle non-finite values.
Results may differ from the reference program's by a relative error of at most 0.019.
Values may be sent and summed in bfloat16 or wider, within the bound.
No kernel may reach another device: no remote copies, remote signals or barrier semaphores. Data moves between devices by JAX's collectives and lax.ppermute only.
A program may use at most 64 MiB of HBM per device.

```python
import jax
import jax.numpy as jnp
from jax import lax

D = 256
HEADS = 4
SYMBOLS = 256
KC = 4
WIN = 256
CTX_DEV = 128
CAP = 8
TILES = 4
NODES = 32768
CTX_ROWS = 16384
SLOTS = 1024
RCAP = 2
N_RANGE = 128


def draw_node_feats(key, part):
    key = jax.random.fold_in(key, 21)
    values = jnp.clip(jax.random.normal(key, (TILES, NODES, D), jnp.float32), -6.0, 6.0)
    return values.astype(jnp.bfloat16)


def draw_w_logit(key, part):
    key = jax.random.fold_in(key, 23)
    values = jnp.clip(0.1875 * jax.random.normal(key, (D, SYMBOLS), jnp.float32), -1.2, 1.2)
    return values.astype(jnp.bfloat16)


def draw_labels(key, part):
    key = jax.random.fold_in(key, 31)
    offset_key, rest_key, order_key = jax.random.split(key, 3)
    windows = TILES * (NODES // WIN)
    offset = jax.random.randint(offset_key, (), 0, SYMBOLS - 1)
    window_ids = jnp.arange(windows, dtype=jnp.int32)
    home = 1 + (offset + window_ids) % (SYMBOLS - 1)
    others = jax.random.randint(rest_key, (windows, WIN), 1, SYMBOLS)
    order_keys = jax.random.split(order_key, windows)
    ranks = jax.vmap(lambda one_key: jax.random.permutation(one_key, WIN))(order_keys)
    chosen = ranks < 3 * WIN // 4
    values = jnp.where(chosen, home[:, None], others)
    return values.reshape(TILES, NODES).astype(jnp.int32)


def draw_ctx_slot(key, part):
    key = jax.random.fold_in(key, 5)
    window_keys = jax.random.split(key, TILES * (NODES // WIN))

    def one_window(window_key):
        return jax.random.permutation(window_key, WIN * KC) % SLOTS
    drawn = jax.vmap(one_window)(window_keys)
    return drawn.reshape(TILES, NODES, KC).astype(jnp.int32)


def draw_relay_slot(key, part):
    key = jax.random.fold_in(key, 9)
    window_keys = jax.random.split(key, TILES * (NODES // WIN))

    def one_window(window_key):
        return jax.random.permutation(window_key, WIN)
    drawn = jax.vmap(one_window)(window_keys)
    return drawn.reshape(TILES, NODES).astype(jnp.int32)


def draw_w_query(key, part):
    key = jax.random.fold_in(key, 13)
    base = jax.random.normal(key, (D, D), jnp.float32) / D ** 0.5
    return base.astype(jnp.bfloat16)


def draw_w_key(key, part):
    key = jax.random.fold_in(key, 17)
    base = jax.random.normal(key, (D, D), jnp.float32) / D ** 0.5
    return base.astype(jnp.bfloat16)


def set_ends(array, rng, least, high):
    spot = [jax.random.randint(jax.random.fold_in(rng, axis), (), 0, length) for axis, length in enumerate(array.shape)]
    widest = array.shape.index(max(array.shape))
    neighbour = spot[:widest] + [(spot[widest] + 1) % array.shape[widest]] + spot[widest + 1:]
    return array.at[tuple(spot)].set(least).at[tuple(neighbour)].set(high)


def level_of(stream_key, extent, shards, least, largest):
    level, own = 1.0, jax.random.fold_in(stream_key, 6)
    for dim, blocks in shards:
        steps = jnp.exp(jax.random.uniform(jax.random.fold_in(own, dim), (blocks,), jnp.float32, least / len(shards), largest / len(shards)))
        level = level * jnp.repeat(steps, extent[dim] // blocks).reshape([-1 if axis == dim else 1 for axis in range(len(extent))])
    return level


def normal_values(rng, extent, width, reach, shards=(), kind=jnp.bfloat16):
    values = jax.random.normal(rng, extent, jnp.float32) * width
    if len(shards) > 0:
        values = level_of(rng, extent, shards, -0.22, 0.18) * values
    return jnp.clip(values, min=-reach, max=reach).astype(kind)


def setup_inputs(seed: int = 0) -> dict:
    keys = jax.random.split(jax.random.key(seed), 15)
    node_feats = draw_node_feats(jax.random.fold_in(keys[14], 71), 0)
    ctx_table = normal_values(keys[1], (TILES, CTX_ROWS, D), 1.0, 6.0, ((0, 4), (1, 128)))
    fetch_rows = set_ends(jax.random.randint(keys[2], (TILES, N_RANGE, N_RANGE, CAP), 0, CTX_DEV), jax.random.fold_in(keys[2], 1), 0, CTX_DEV - 1).astype(jnp.int32)
    ctx_slot = draw_ctx_slot(jax.random.fold_in(keys[14], 71), 0)
    labels = draw_labels(jax.random.fold_in(keys[14], 71), 0)
    relay_slot = draw_relay_slot(jax.random.fold_in(keys[14], 71), 0)
    w_ctx = normal_values(keys[6], (KC * D, D), (KC * D) ** -0.5, 0.1875)
    w_query = draw_w_query(jax.random.fold_in(keys[14], 71), 0)
    w_key = draw_w_key(jax.random.fold_in(keys[14], 71), 0)
    w_value = normal_values(keys[9], (D, D), D ** -0.5, 0.375)
    w_proj = normal_values(keys[10], (D, D), D ** -0.5, 0.375)
    w_logit = draw_w_logit(jax.random.fold_in(keys[14], 71), 0)
    gain_attn = jnp.clip(1.0 + 0.12 * jax.random.normal(keys[12], (D,), jnp.float32), 0.4, 1.6)
    gain_out = jnp.clip(1.0 + 0.12 * jax.random.normal(keys[13], (D,), jnp.float32), 0.4, 1.6)
    return {"node_feats": node_feats, "ctx_table": ctx_table, "fetch_rows": fetch_rows, "ctx_slot": ctx_slot, "labels": labels, "relay_slot": relay_slot, "w_ctx": w_ctx, "w_query": w_query, "w_key": w_key, "w_value": w_value, "w_proj": w_proj, "w_logit": w_logit, "gain_attn": gain_attn, "gain_out": gain_out}


def rms_scale(inputs, gain_vec):
    return inputs * lax.rsqrt(lax.optimization_barrier(jnp.mean(inputs * inputs, axis=-1, keepdims=True)) + 1e-06) * gain_vec

def window_loss(weights, features, contexts, targets):
    w_ctx, w_query, w_key, w_value, w_proj, w_logit, gain_attn, gain_out = weights
    length = features.shape[0]
    hidden_start = features.astype(jnp.float32) + jnp.dot(contexts, w_ctx, preferred_element_type=jnp.float32)
    normed = rms_scale(hidden_start, gain_attn).astype(jnp.bfloat16)
    queries = jnp.dot(normed, w_query, preferred_element_type=jnp.float32).astype(jnp.bfloat16).reshape(length, HEADS, -1)
    key_rows = jnp.dot(normed, w_key, preferred_element_type=jnp.float32).astype(jnp.bfloat16).reshape(length, HEADS, -1)
    value_rows = jnp.dot(normed, w_value, preferred_element_type=jnp.float32).astype(jnp.bfloat16).reshape(length, HEADS, -1)
    scale_factor = 1.0 / queries.shape[-1] ** 0.5
    scores = jnp.einsum('qhd,khd->hqk', queries.astype(jnp.float32), key_rows.astype(jnp.float32)) * scale_factor
    causal = lax.broadcasted_iota(jnp.int32, (length, length), 0) >= lax.broadcasted_iota(jnp.int32, (length, length), 1)
    scores = jnp.where(causal[None], scores, -1e+30)
    row_max = lax.optimization_barrier(jnp.max(scores, axis=-1, keepdims=True))
    expo = jnp.exp(scores - row_max)
    probabilities = (expo / lax.optimization_barrier(jnp.sum(expo, axis=-1, keepdims=True))).astype(jnp.bfloat16)
    attended = jnp.einsum('hqk,khd->qhd', probabilities.astype(jnp.float32), value_rows.astype(jnp.float32))
    attended = attended.reshape(length, -1).astype(jnp.bfloat16)
    hidden_end = hidden_start + jnp.dot(attended, w_proj, preferred_element_type=jnp.float32)
    normed_out = rms_scale(hidden_end, gain_out).astype(jnp.bfloat16)
    logits = jnp.dot(normed_out, w_logit, preferred_element_type=jnp.float32)
    logit_max = lax.optimization_barrier(jnp.max(logits, axis=-1, keepdims=True))
    log_total = logit_max[:, 0] + jnp.log(lax.optimization_barrier(jnp.sum(jnp.exp(logits - logit_max), axis=-1)))
    picked = jnp.take_along_axis(logits, targets[:, None], axis=1)[:, 0]
    return (jnp.sum(log_total - picked), hidden_end.astype(jnp.bfloat16))

def window_step(weights, features, contexts, targets, node_total):

    def objective(params):
        loss_sum, relay_rows = window_loss(params, features, contexts, targets)
        return (loss_sum / node_total, relay_rows)
    loss_value, pullback, relay_rows = jax.vjp(objective, weights, has_aux=True)
    gradients = pullback(jnp.ones_like(loss_value))[0]
    gradients = tuple((grad_item.astype(jnp.float32) for grad_item in gradients))
    return (loss_value, gradients, relay_rows)

def reference(node_feats, ctx_table, fetch_rows, ctx_slot, labels, relay_slot, w_ctx, w_query, w_key, w_value, w_proj, w_logit, gain_attn, gain_out):
    weights = (w_ctx, w_query, w_key, w_value, w_proj, w_logit, gain_attn, gain_out)
    node_total = float(TILES * NODES)
    owner_base = (jnp.arange(N_RANGE, dtype=jnp.int32) * CTX_DEV)[:, None]

    def one_window(running, window_id):
        tile_id = window_id // N_RANGE
        range_id = window_id % N_RANGE
        first_node = (range_id * WIN).astype(jnp.int32)
        features = lax.dynamic_slice_in_dim(node_feats[tile_id], first_node, WIN, 0)
        wanted = (owner_base + fetch_rows[tile_id, range_id]).reshape(-1).astype(jnp.int32)
        buffer = ctx_table[tile_id][wanted]
        slot_ids = lax.dynamic_slice_in_dim(ctx_slot[tile_id], first_node, WIN, 0)
        contexts = buffer[slot_ids].reshape(WIN, KC * D)
        targets = lax.dynamic_slice_in_dim(labels[tile_id], first_node, WIN, 0)
        loss_value, gradients, relay_rows = window_step(weights, features, contexts, targets, node_total)
        loss_run, grad_run = running
        grad_run = tuple((old_sum + new_term for old_sum, new_term in zip(grad_run, gradients)))
        return ((loss_run + loss_value, grad_run), relay_rows)
    zero_grads = tuple((jnp.zeros(weight_item.shape, jnp.float32) for weight_item in weights))
    start_state = (jnp.zeros((), jnp.float32), zero_grads)
    (loss_total, gradients), hidden_all = lax.scan(one_window, start_state, jnp.arange(TILES * N_RANGE, dtype=jnp.int32))
    hidden_all = hidden_all.reshape(TILES, NODES, D)
    source = (jnp.arange(NODES, dtype=jnp.int32) // WIN)[None, :]
    dest_rows = relay_slot // RCAP * WIN + source * RCAP + relay_slot % RCAP

    def place_tile(tile_rows, tile_dest):
        return jnp.zeros((NODES, D), jnp.bfloat16).at[tile_dest].set(tile_rows)
    relayed = jax.vmap(place_tile)(hidden_all, dest_rows)
    grad_ctx, grad_query, grad_key, grad_value, grad_proj, grad_logit, grad_gain_attn, grad_gain_out = gradients
    return (relayed, loss_total, grad_ctx, grad_query, grad_key, grad_value, grad_proj, grad_logit, grad_gain_attn, grad_gain_out)
```

```python
import functools

import jax
import jax.numpy as jnp
from jax import lax
from jax.experimental import pallas as pl
from jax.experimental.pallas import tpu as pltpu
from jax.sharding import PartitionSpec as P

HEADS = 4
F32 = jnp.float32
BF16 = jnp.bfloat16


def nn(a, b):
    return lax.dot_general(a, b, (((1,), (0,)), ((), ())), preferred_element_type=F32)


def nt(a, b):
    return lax.dot_general(a, b, (((1,), (1,)), ((), ())), preferred_element_type=F32)


def tn(a, b):
    return lax.dot_general(a, b, (((0,), (0,)), ((), ())), preferred_element_type=F32)


def pick_kernel(idx_ref, table_ref, out_ref):
    asks, cap = idx_ref.shape
    rows = asks * cap
    table_rows = table_ref.shape[0]
    line = lax.broadcasted_iota(jnp.int32, (rows, asks), 0)
    spread = (line // cap == lax.broadcasted_iota(jnp.int32, (rows, asks), 1)).astype(BF16)
    ids = nn(spread, idx_ref[...].astype(F32).astype(BF16))
    own = lax.broadcasted_iota(jnp.int32, (rows, cap), 0) % cap == lax.broadcasted_iota(
        jnp.int32, (rows, cap), 1
    )
    ids = jnp.sum(jnp.where(own, ids, 0.0), axis=1, keepdims=True).astype(jnp.int32)
    hot = (ids == lax.broadcasted_iota(jnp.int32, (rows, table_rows), 1)).astype(BF16)
    out_ref[...] = nn(hot, table_ref[...]).astype(BF16)


def step_kernel(
    node_total,
    share,
    core_ref,
    feats_ref,
    buf_ref,
    slot_ref,
    label_ref,
    relay_ref,
    w_ctx_ref,
    w_query_ref,
    w_key_ref,
    w_value_ref,
    w_proj_ref,
    w_logit_ref,
    gain_attn_ref,
    gain_out_ref,
    keep_ref,
    send_ref,
    relayed_ref,
    ids_ref,
    slab_ref,
    extra_ref,
    prob_ref,
    sems,
):
    length, width = feats_ref.shape
    slots = buf_ref.shape[0]
    kc = slot_ref.shape[0]
    head_width = width // HEADS

    ids_ref[0:kc, :] = slot_ref[...]
    ids_ref[kc : kc + 1, :] = label_ref[...]
    ids_ref[kc + 1 :, :] = jnp.zeros((8 - kc - 1, length), jnp.int32)
    ids = jnp.transpose(ids_ref[...])

    buf = buf_ref[...]
    slot_lane = lax.broadcasted_iota(jnp.int32, (length, slots), 1)
    contexts = []
    hidden0 = feats_ref[...].astype(F32)
    for k in range(kc):
        hot = (ids[:, k : k + 1] == slot_lane).astype(BF16)
        part = nn(hot, buf).astype(BF16)
        contexts.append(part)
        hidden0 = hidden0 + nn(part, w_ctx_ref[k * width : (k + 1) * width, :])

    gain_attn = gain_attn_ref[...]
    inv1 = lax.rsqrt(jnp.mean(hidden0 * hidden0, axis=1, keepdims=True) + 1e-06)
    unit1 = hidden0 * inv1
    normed = (unit1 * gain_attn).astype(BF16)
    queries = nn(normed, w_query_ref[...]).astype(BF16)
    key_rows = nn(normed, w_key_ref[...]).astype(BF16)
    value_rows = nn(normed, w_value_ref[...]).astype(BF16)

    lane_head = lax.broadcasted_iota(jnp.int32, (length, width), 1) // head_width
    causal = lax.broadcasted_iota(jnp.int32, (length, length), 0) >= lax.broadcasted_iota(
        jnp.int32, (length, length), 1
    )
    scale = 1.0 / head_width**0.5

    def of_head(rows, h):
        return jnp.where(lane_head == h, rows, jnp.zeros_like(rows))

    attended = jnp.zeros((length, width), F32)
    for h in range(HEADS):
        scores = nt(of_head(queries, h), key_rows) * scale
        scores = jnp.where(causal, scores, -1e30)
        expo = jnp.exp(scores - jnp.max(scores, axis=1, keepdims=True))
        prob = expo / jnp.sum(expo, axis=1, keepdims=True)
        prob_ref[h] = prob
        attended = attended + nn(prob.astype(BF16), of_head(value_rows, h))
    attended = attended.astype(BF16)
    hidden1 = hidden0 + nn(attended, w_proj_ref[...])

    line = lax.broadcasted_iota(jnp.int32, (2 * length, length), 0)
    place = relay_ref[...] == line // (2 * share) * share + line % share
    moved = nn(place.astype(BF16), hidden1.astype(BF16))
    line = lax.broadcasted_iota(jnp.int32, (2 * length, 128), 0)
    left = line // share % 2 == 0
    relayed_ref[...] = jnp.where(left, moved[:, :128], moved[:, 128:]).astype(BF16)

    gain_out = gain_out_ref[...]
    inv2 = lax.rsqrt(jnp.mean(hidden1 * hidden1, axis=1, keepdims=True) + 1e-06)
    unit2 = hidden1 * inv2
    normed_out = (unit2 * gain_out).astype(BF16)
    logits = nn(normed_out, w_logit_ref[...])
    symbol = lax.broadcasted_iota(jnp.int32, logits.shape, 1)
    target = symbol == ids[:, kc : kc + 1]
    logit_max = jnp.max(logits, axis=1, keepdims=True)
    expo = jnp.exp(logits - logit_max)
    total = jnp.sum(expo, axis=1, keepdims=True)
    picked = jnp.sum(jnp.where(target, logits, 0.0), axis=1, keepdims=True)
    losses = logit_max + jnp.log(total) - picked
    loss = jnp.sum(losses, axis=0, keepdims=True) * (1.0 / node_total)

    g_logits = ((expo / total - target.astype(F32)) * (1.0 / node_total)).astype(BF16)
    g_w_logit = tn(normed_out, g_logits).astype(BF16)
    g_normed_out = nt(g_logits, w_logit_ref[...]).astype(BF16).astype(F32)
    g_gain_out = jnp.sum(g_normed_out * unit2, axis=0, keepdims=True)
    g_unit = g_normed_out * gain_out
    g_hidden1 = inv2 * (g_unit - unit2 * jnp.mean(g_unit * unit2, axis=1, keepdims=True))
    g_rows = g_hidden1.astype(BF16)
    g_w_proj = tn(attended, g_rows).astype(BF16)
    g_attended = nt(g_rows, w_proj_ref[...]).astype(BF16)

    g_queries = jnp.zeros((length, width), F32)
    g_keys = jnp.zeros((length, width), F32)
    g_values = jnp.zeros((length, width), F32)
    for h in range(HEADS):
        prob = prob_ref[h]
        g_att_h = of_head(g_attended, h)
        g_prob = nt(g_att_h, value_rows).astype(BF16).astype(F32)
        g_values = g_values + tn(prob.astype(BF16), g_att_h)
        weighed = jnp.sum(g_prob * prob, axis=1, keepdims=True)
        g_scores = (prob * (g_prob - weighed) * scale).astype(BF16)
        g_queries = g_queries + nn(g_scores, of_head(key_rows, h))
        g_keys = g_keys + tn(g_scores, of_head(queries, h))
    g_queries = g_queries.astype(BF16)
    g_keys = g_keys.astype(BF16)
    g_values = g_values.astype(BF16)
    g_w_query = tn(normed, g_queries).astype(BF16)
    g_w_key = tn(normed, g_keys).astype(BF16)
    g_w_value = tn(normed, g_values).astype(BF16)
    g_normed = (
        nt(g_queries, w_query_ref[...])
        + nt(g_keys, w_key_ref[...])
        + nt(g_values, w_value_ref[...])
    )
    g_gain_attn = jnp.sum(g_normed * unit1, axis=0, keepdims=True)
    g_unit = g_normed * gain_attn
    g_hidden0 = g_hidden1 + inv1 * (
        g_unit - unit1 * jnp.mean(g_unit * unit1, axis=1, keepdims=True)
    )
    g_rows = g_hidden0.astype(BF16)
    for k in range(kc):
        g_w_ctx = tn(contexts[k], g_rows).astype(BF16)
        slab_ref[0, k * width : (k + 1) * width, :] = g_w_ctx[:, :128]
        slab_ref[0, (kc + k) * width : (kc + k + 1) * width, :] = g_w_ctx[:, 128:]
    first = 2 * kc * width
    slab_ref[0, first : first + width, :] = g_w_logit[:, :128]
    slab_ref[1, 0:width, :] = g_w_logit[:, 128:]
    row = width
    for grad in (g_w_query, g_w_key, g_w_value, g_w_proj):
        slab_ref[1, row : row + width, :] = grad[:, :128]
        slab_ref[1, row + width : row + 2 * width, :] = grad[:, 128:]
        row += 2 * width
    extra_ref[...] = jnp.zeros_like(extra_ref)
    extra_ref[0:1, :] = g_gain_attn[:, :128]
    extra_ref[1:2, :] = g_gain_attn[:, 128:]
    extra_ref[2:3, :] = g_gain_out[:, :128]
    extra_ref[3:4, :] = g_gain_out[:, 128:]
    extra_ref[4:5, :] = jnp.broadcast_to(loss, (1, 128))
    used = first + width
    slab_ref[0, used : used + 16, :] = extra_ref[...].astype(BF16)
    half = slab_ref.shape[1]
    slab_ref[0, used + 16 :, :] = jnp.zeros((half - used - 16, 128), BF16)
    slab_ref[1, used:, :] = jnp.zeros((half - used, 128), BF16)

    core = core_ref[0]
    keep = pltpu.make_async_copy(slab_ref.at[core], keep_ref, sems.at[0])
    send = pltpu.make_async_copy(slab_ref.at[1 - core], send_ref, sems.at[1])
    keep.start()
    send.start()
    keep.wait()
    send.wait()


def unpack_kernel(
    share,
    core_ref,
    own_ref,
    own_rows_ref,
    other_ref,
    relayed_ref,
    ctx_ref,
    query_ref,
    key_ref,
    value_ref,
    proj_ref,
    logit_ref,
    attn_ref,
    out_ref,
    loss_ref,
):
    core = core_ref[0]
    rows = ctx_ref.shape[0]
    width = logit_ref.shape[0]
    half = own_ref.shape[0]

    def lines(h, start, count):
        mine = own_ref[start : start + count, :].astype(F32)
        theirs = other_ref[start : start + count, :].astype(F32)
        return jnp.where(core == h, mine, theirs)

    for row in range(0, rows, width):
        ctx_ref[row : row + width, :128] = lines(0, row, width)
        ctx_ref[row : row + width, 128:] = lines(0, rows + row, width)
    logit_ref[:, :128] = lines(0, 2 * rows, width)
    logit_ref[:, 128:] = lines(1, 0, width)
    row = width
    for ref in (query_ref, key_ref, value_ref, proj_ref):
        ref[:, :128] = lines(1, row, width)
        ref[:, 128:] = lines(1, row + width, width)
        row += 2 * width
    extra = lines(0, 2 * rows + width, 16)
    attn_ref[:, :128] = extra[0:1]
    attn_ref[:, 128:] = extra[1:2]
    out_ref[:, :128] = extra[2:3]
    out_ref[:, 128:] = extra[3:4]
    loss_ref[...] = extra[4:5, 0:1]

    length = relayed_ref.shape[0]
    row = lax.broadcasted_iota(jnp.int32, (length, 2 * length), 0)
    line = lax.broadcasted_iota(jnp.int32, (length, 2 * length), 1)
    mine = row // share % 2 == core
    own_rows = own_rows_ref[...]
    other_rows = other_ref[half:, :]
    for h in range(2):
        found = line == (row // (2 * share) * 4 + 2 * core + h) * share + row % share
        here = (found & mine).astype(BF16)
        there = (found & ~mine).astype(BF16)
        relayed_ref[:, h * 128 : (h + 1) * 128] = (
            nn(here, own_rows) + nn(there, other_rows)
        ).astype(BF16)


def body(
    node_feats,
    ctx_table,
    fetch_rows,
    ctx_slot,
    labels,
    relay_slot,
    w_ctx,
    w_query,
    w_key,
    w_value,
    w_proj,
    w_logit,
    gain_attn,
    gain_out,
):
    features = node_feats[0]
    length, width = features.shape
    ranges = lax.axis_size("range")
    table = ctx_table[0]
    requests = fetch_rows[0, 0]
    cap = requests.shape[1]
    tiles = lax.axis_size("dp")
    chips = ranges // 2
    share = length // ranges
    core = (lax.axis_index("range") % 2).astype(jnp.int32).reshape(1)
    half = (w_ctx.shape[0] * width + 5 * width * width) // 256 + 16
    half = -(-half // (2 * tiles * chips)) * (2 * tiles * chips)
    quarter = half // tiles
    pairs = quarter // (2 * chips)
    relay_pairs = length // chips
    vmem = pl.BlockSpec(memory_space=pltpu.VMEM)
    params = pltpu.CompilerParams(vmem_limit_bytes=32 * 1024 * 1024)

    asked = lax.all_to_all(requests, "range", split_axis=0, concat_axis=0, tiled=True)
    picked = pl.pallas_call(
        pick_kernel,
        out_shape=jax.ShapeDtypeStruct((ranges * cap, width), BF16),
        in_specs=[vmem] * 2,
        out_specs=vmem,
        compiler_params=params,
        name="pick_rows",
    )(asked, table)
    buffer = lax.all_to_all(
        picked.reshape(ranges, cap, width), "range", split_axis=0, concat_axis=0, tiled=True
    ).reshape(ranges * cap, width)

    smem = pl.BlockSpec(memory_space=pltpu.SMEM)
    anywhere = pl.BlockSpec(memory_space=pl.ANY)
    keep, send, moved = pl.pallas_call(
        functools.partial(step_kernel, float(length * ranges * tiles), share),
        out_shape=(
            jax.ShapeDtypeStruct((half, 128), BF16),
            jax.ShapeDtypeStruct((half, 128), BF16),
            jax.ShapeDtypeStruct((2 * length, 128), BF16),
        ),
        in_specs=[smem] + [vmem] * 13,
        out_specs=(anywhere, anywhere, vmem),
        scratch_shapes=[
            pltpu.VMEM((8, length), jnp.int32),
            pltpu.VMEM((2, half, 128), BF16),
            pltpu.VMEM((16, 128), F32),
            pltpu.VMEM((HEADS, length, length), F32),
            pltpu.SemaphoreType.DMA((2,)),
        ],
        compiler_params=params,
        name="window_step",
    )(
        core,
        features,
        buffer,
        jnp.transpose(ctx_slot[0]),
        labels,
        relay_slot,
        w_ctx,
        w_query,
        w_key,
        w_value,
        w_proj,
        w_logit,
        gain_attn.reshape(1, width),
        gain_out.reshape(1, width),
    )

    swap = [(i, i ^ 1) for i in range(ranges)]
    same_core = [list(range(c, ranges, 2)) for c in range(2)]
    other = lax.ppermute(send, "range", swap)
    pair = (keep.astype(F32) + other.astype(F32)).astype(BF16)
    parts = lax.all_to_all(
        pair.reshape(tiles, quarter, 128), "dp", split_axis=0, concat_axis=0, tiled=True
    )
    part = jnp.sum(parts.astype(F32), axis=0).astype(BF16)
    parts = lax.all_to_all(
        part.reshape(chips, pairs, 2, 128),
        "range",
        split_axis=0,
        concat_axis=0,
        tiled=True,
        axis_index_groups=same_core,
    )
    piece = jnp.sum(parts.astype(F32), axis=0).astype(BF16)

    outgoing = jnp.concatenate(
        [
            jnp.broadcast_to(piece[None], (chips, pairs, 2, 128)),
            moved.reshape(chips, relay_pairs, 2, 128),
        ],
        axis=1,
    )
    incoming = lax.all_to_all(
        outgoing,
        "range",
        split_axis=0,
        concat_axis=0,
        tiled=True,
        axis_index_groups=same_core,
    )
    part = incoming[:, :pairs].reshape(1, quarter, 128)
    own_rows = incoming[:, pairs:].reshape(2 * length, 128)
    own = lax.all_to_all(
        jnp.broadcast_to(part, (tiles, quarter, 128)),
        "dp",
        split_axis=0,
        concat_axis=0,
        tiled=True,
    ).reshape(half, 128)
    other = lax.ppermute(jnp.concatenate([own, own_rows], axis=0), "range", swap)

    square = jax.ShapeDtypeStruct((width, width), F32)
    line = jax.ShapeDtypeStruct((1, width), F32)
    outs = pl.pallas_call(
        functools.partial(unpack_kernel, share),
        out_shape=(
            jax.ShapeDtypeStruct((length, width), BF16),
            jax.ShapeDtypeStruct(w_ctx.shape, F32),
        )
        + (square,) * 5
        + (line, line, jax.ShapeDtypeStruct((1, 1), F32)),
        in_specs=[smem] + [vmem] * 3,
        out_specs=(vmem,) * 10,
        compiler_params=params,
        name="unpack",
    )(core, own, own_rows, other)
    return (
        outs[0][None],
        outs[9].reshape(()),
        outs[1],
        outs[2],
        outs[3],
        outs[4],
        outs[5],
        outs[6],
        outs[7].reshape(width),
        outs[8].reshape(width),
    )


def solution(mesh):
    placed = (
        P("dp", "range", None),
        P("dp", "range", None),
        P("dp", "range", None, None),
        P("dp", "range", None),
        P("dp", "range"),
        P("dp", "range"),
        P(),
        P(),
        P(),
        P(),
        P(),
        P(),
        P(),
        P(),
    )
    return jax.shard_map(
        body,
        mesh=mesh,
        in_specs=placed,
        out_specs=(P("dp", "range", None), P(), P(), P(), P(), P(), P(), P(), P(), P()),
        check_vma=False,
    )
```

```python
import functools

import jax
import jax.numpy as jnp
from jax import lax
from jax.experimental import pallas as pl
from jax.experimental.pallas import tpu as pltpu
from jax.sharding import PartitionSpec as P

HEADS = 4
F32 = jnp.float32
BF16 = jnp.bfloat16


def nn(a, b):
    return lax.dot_general(a, b, (((1,), (0,)), ((), ())), preferred_element_type=F32)


def nt(a, b):
    return lax.dot_general(a, b, (((1,), (1,)), ((), ())), preferred_element_type=F32)


def tn(a, b):
    return lax.dot_general(a, b, (((0,), (0,)), ((), ())), preferred_element_type=F32)


def ask_kernel(asks_ref, table_ref, out_ref, held_ref):
    cap, owners = asks_ref.shape
    lines = jnp.concatenate([asks_ref[...], jnp.zeros((128 - cap, owners), jnp.int32)], axis=0)
    out_ref[...] = jnp.transpose(lines)
    held_ref[...] = table_ref[...]


def pick_kernel(idx_ref, table_ref, out_ref):
    asks, lanes = idx_ref.shape
    rows = out_ref.shape[0]
    cap = rows // asks
    table_rows = table_ref.shape[0]
    line = lax.broadcasted_iota(jnp.int32, (rows, asks), 0)
    spread = (line // cap == lax.broadcasted_iota(jnp.int32, (rows, asks), 1)).astype(BF16)
    ids = nn(spread, idx_ref[...].astype(F32).astype(BF16))
    own = lax.broadcasted_iota(jnp.int32, (rows, lanes), 0) % cap == lax.broadcasted_iota(
        jnp.int32, (rows, lanes), 1
    )
    ids = jnp.sum(jnp.where(own, ids, 0.0), axis=1, keepdims=True).astype(jnp.int32)
    hot = (ids == lax.broadcasted_iota(jnp.int32, (rows, table_rows), 1)).astype(BF16)
    out_ref[...] = nn(hot, table_ref[...]).astype(BF16)


def step_kernel(
    node_total,
    share,
    core_ref,
    feats_ref,
    buf_ref,
    slot_ref,
    label_ref,
    relay_ref,
    w_ctx_ref,
    w_query_ref,
    w_key_ref,
    w_value_ref,
    w_proj_ref,
    w_logit_ref,
    gain_attn_ref,
    gain_out_ref,
    keep_ref,
    send_ref,
    relayed_ref,
    ids_ref,
    slab_ref,
    extra_ref,
    prob_ref,
    sems,
):
    length, width = feats_ref.shape
    slots = buf_ref.shape[0]
    kc = slot_ref.shape[0]
    head_width = width // HEADS

    ids_ref[0:kc, :] = slot_ref[...]
    ids_ref[kc : kc + 1, :] = label_ref[...]
    ids_ref[kc + 1 :, :] = jnp.zeros((8 - kc - 1, length), jnp.int32)
    ids = jnp.transpose(ids_ref[...])

    buf = buf_ref[...]
    slot_lane = lax.broadcasted_iota(jnp.int32, (length, slots), 1)
    contexts = []
    hidden0 = feats_ref[...].astype(F32)
    for k in range(kc):
        hot = (ids[:, k : k + 1] == slot_lane).astype(BF16)
        part = nn(hot, buf).astype(BF16)
        contexts.append(part)
        hidden0 = hidden0 + nn(part, w_ctx_ref[k * width : (k + 1) * width, :])

    gain_attn = gain_attn_ref[...]
    inv1 = lax.rsqrt(jnp.mean(hidden0 * hidden0, axis=1, keepdims=True) + 1e-06)
    unit1 = hidden0 * inv1
    normed = (unit1 * gain_attn).astype(BF16)
    queries = nn(normed, w_query_ref[...]).astype(BF16)
    key_rows = nn(normed, w_key_ref[...]).astype(BF16)
    value_rows = nn(normed, w_value_ref[...]).astype(BF16)

    lane_head = lax.broadcasted_iota(jnp.int32, (length, width), 1) // head_width
    causal = lax.broadcasted_iota(jnp.int32, (length, length), 0) >= lax.broadcasted_iota(
        jnp.int32, (length, length), 1
    )
    scale = 1.0 / head_width**0.5

    def of_head(rows, h):
        return jnp.where(lane_head == h, rows, jnp.zeros_like(rows))

    attended = jnp.zeros((length, width), F32)
    for h in range(HEADS):
        scores = nt(of_head(queries, h), key_rows) * scale
        scores = jnp.where(causal, scores, -1e30)
        expo = jnp.exp(scores - jnp.max(scores, axis=1, keepdims=True))
        prob = expo / jnp.sum(expo, axis=1, keepdims=True)
        prob_ref[h] = prob
        attended = attended + nn(prob.astype(BF16), of_head(value_rows, h))
    attended = attended.astype(BF16)
    hidden1 = hidden0 + nn(attended, w_proj_ref[...])

    line = lax.broadcasted_iota(jnp.int32, (2 * length, length), 0)
    place = relay_ref[...] == line // (2 * share) * share + line % share
    moved = nn(place.astype(BF16), hidden1.astype(BF16))
    line = lax.broadcasted_iota(jnp.int32, (2 * length, 128), 0)
    left = line // share % 2 == 0
    relayed_ref[...] = jnp.where(left, moved[:, :128], moved[:, 128:]).astype(BF16)

    gain_out = gain_out_ref[...]
    inv2 = lax.rsqrt(jnp.mean(hidden1 * hidden1, axis=1, keepdims=True) + 1e-06)
    unit2 = hidden1 * inv2
    normed_out = (unit2 * gain_out).astype(BF16)
    logits = nn(normed_out, w_logit_ref[...])
    symbol = lax.broadcasted_iota(jnp.int32, logits.shape, 1)
    target = symbol == ids[:, kc : kc + 1]
    logit_max = jnp.max(logits, axis=1, keepdims=True)
    expo = jnp.exp(logits - logit_max)
    total = jnp.sum(expo, axis=1, keepdims=True)
    picked = jnp.sum(jnp.where(target, logits, 0.0), axis=1, keepdims=True)
    losses = logit_max + jnp.log(total) - picked
    lane = lax.broadcasted_iota(jnp.int32, (length, 128), 1)
    own_lane = lax.broadcasted_iota(jnp.int32, (length, 128), 0) % 128 == lane
    loss = jnp.sum(jnp.where(own_lane, losses, 0.0), axis=0, keepdims=True) * (1.0 / node_total)

    g_logits = ((expo / total - target.astype(F32)) * (1.0 / node_total)).astype(BF16)
    g_w_logit = tn(normed_out, g_logits).astype(BF16)
    g_normed_out = nt(g_logits, w_logit_ref[...]).astype(BF16).astype(F32)
    g_gain_out = jnp.sum(g_normed_out * unit2, axis=0, keepdims=True)
    g_unit = g_normed_out * gain_out
    g_hidden1 = inv2 * (g_unit - unit2 * jnp.mean(g_unit * unit2, axis=1, keepdims=True))
    g_rows = g_hidden1.astype(BF16)
    g_w_proj = tn(attended, g_rows).astype(BF16)
    g_attended = nt(g_rows, w_proj_ref[...]).astype(BF16)

    g_queries = jnp.zeros((length, width), F32)
    g_keys = jnp.zeros((length, width), F32)
    g_values = jnp.zeros((length, width), F32)
    for h in range(HEADS):
        prob = prob_ref[h]
        g_att_h = of_head(g_attended, h)
        g_prob = nt(g_att_h, value_rows).astype(BF16).astype(F32)
        g_values = g_values + tn(prob.astype(BF16), g_att_h)
        weighed = jnp.sum(g_prob * prob, axis=1, keepdims=True)
        g_scores = (prob * (g_prob - weighed) * scale).astype(BF16)
        g_queries = g_queries + nn(g_scores, of_head(key_rows, h))
        g_keys = g_keys + tn(g_scores, of_head(queries, h))
    g_queries = g_queries.astype(BF16)
    g_keys = g_keys.astype(BF16)
    g_values = g_values.astype(BF16)
    g_w_query = tn(normed, g_queries).astype(BF16)
    g_w_key = tn(normed, g_keys).astype(BF16)
    g_w_value = tn(normed, g_values).astype(BF16)
    g_normed = (
        nt(g_queries, w_query_ref[...])
        + nt(g_keys, w_key_ref[...])
        + nt(g_values, w_value_ref[...])
    )
    g_gain_attn = jnp.sum(g_normed * unit1, axis=0, keepdims=True)
    g_unit = g_normed * gain_attn
    g_hidden0 = g_hidden1 + inv1 * (
        g_unit - unit1 * jnp.mean(g_unit * unit1, axis=1, keepdims=True)
    )
    g_rows = g_hidden0.astype(BF16)
    for k in range(kc):
        g_w_ctx = tn(contexts[k], g_rows).astype(BF16)
        slab_ref[0, k * width : (k + 1) * width, :] = g_w_ctx[:, :128]
        slab_ref[0, (kc + k) * width : (kc + k + 1) * width, :] = g_w_ctx[:, 128:]
    first = 2 * kc * width
    slab_ref[0, first : first + width, :] = g_w_logit[:, :128]
    slab_ref[1, 0:width, :] = g_w_logit[:, 128:]
    row = width
    for grad in (g_w_query, g_w_key, g_w_value, g_w_proj):
        slab_ref[1, row : row + width, :] = grad[:, :128]
        slab_ref[1, row + width : row + 2 * width, :] = grad[:, 128:]
        row += 2 * width
    extra_ref[...] = jnp.zeros_like(extra_ref)
    extra_ref[0:1, :] = g_gain_attn[:, :128]
    extra_ref[1:2, :] = g_gain_attn[:, 128:]
    extra_ref[2:3, :] = g_gain_out[:, :128]
    extra_ref[3:4, :] = g_gain_out[:, 128:]
    extra_ref[4:5, :] = loss
    used = first + width
    slab_ref[0, used : used + 16, :] = extra_ref[...].astype(BF16)
    half = slab_ref.shape[1]
    slab_ref[0, used + 16 :, :] = jnp.zeros((half - used - 16, 128), BF16)
    slab_ref[1, used:, :] = jnp.zeros((half - used, 128), BF16)

    core = core_ref[0]
    keep = pltpu.make_async_copy(slab_ref.at[core], keep_ref, sems.at[0])
    send = pltpu.make_async_copy(slab_ref.at[1 - core], send_ref, sems.at[1])
    keep.start()
    send.start()
    keep.wait()
    send.wait()


def unpack_kernel(
    share,
    side,
    core_ref,
    own_ref,
    own_rows_ref,
    other_ref,
    relayed_ref,
    ctx_ref,
    query_ref,
    key_ref,
    value_ref,
    proj_ref,
    logit_ref,
    attn_ref,
    out_ref,
    loss_ref,
):
    core = core_ref[0]
    rows = ctx_ref.shape[0]
    width = logit_ref.shape[0]
    half = own_ref.shape[0]

    def lines(h, start, count):
        mine = own_ref[start : start + count, :].astype(F32)
        theirs = other_ref[start : start + count, :].astype(F32)
        return jnp.where(core == h, mine, theirs)

    for row in range(0, rows, width):
        ctx_ref[row : row + width, :128] = lines(0, row, width)
        ctx_ref[row : row + width, 128:] = lines(0, rows + row, width)
    logit_ref[:, :128] = lines(0, 2 * rows, width)
    logit_ref[:, 128:] = lines(1, 0, width)
    row = width
    for ref in (query_ref, key_ref, value_ref, proj_ref):
        ref[:, :128] = lines(1, row, width)
        ref[:, 128:] = lines(1, row + width, width)
        row += 2 * width
    extra = lines(0, 2 * rows + width, 16)
    attn_ref[:, :128] = extra[0:1]
    attn_ref[:, 128:] = extra[1:2]
    out_ref[:, :128] = extra[2:3]
    out_ref[:, 128:] = extra[3:4]
    loss_ref[...] = jnp.sum(extra[4:5], axis=1, keepdims=True)

    length = relayed_ref.shape[0]
    row = lax.broadcasted_iota(jnp.int32, (length, 2 * length), 0)
    line = lax.broadcasted_iota(jnp.int32, (length, 2 * length), 1)
    mine = row // share % 2 == core
    chip = row // (2 * share)
    chip = chip % side * side + chip // side
    own_rows = own_rows_ref[...]
    other_rows = other_ref[half:, :]
    for h in range(2):
        found = line == (chip * 4 + 2 * core + h) * share + row % share
        here = (found & mine).astype(BF16)
        there = (found & ~mine).astype(BF16)
        relayed_ref[:, h * 128 : (h + 1) * 128] = (
            nn(here, own_rows) + nn(there, other_rows)
        ).astype(BF16)


def body(
    node_feats,
    ctx_table,
    fetch_rows,
    ctx_slot,
    labels,
    relay_slot,
    w_ctx,
    w_query,
    w_key,
    w_value,
    w_proj,
    w_logit,
    gain_attn,
    gain_out,
):
    features = node_feats[0]
    length, width = features.shape
    ranges = lax.axis_size("range")
    table = ctx_table[0]
    requests = fetch_rows[0, 0]
    cap = requests.shape[1]
    tiles = lax.axis_size("dp")
    chips = ranges // 2
    side = round(chips**0.5)
    share = length // ranges
    core = (lax.axis_index("range") % 2).astype(jnp.int32).reshape(1)
    half = (w_ctx.shape[0] * width + 5 * width * width) // 256 + 16
    half = -(-half // (16 * tiles * side)) * (16 * tiles * side)
    quarter = half // tiles
    piece_rows = quarter // side
    moved_rows = 2 * length // side
    vmem = pl.BlockSpec(memory_space=pltpu.VMEM)
    params = pltpu.CompilerParams(vmem_limit_bytes=32 * 1024 * 1024)

    asks, held = pl.pallas_call(
        ask_kernel,
        out_shape=(
            jax.ShapeDtypeStruct((ranges, 128), jnp.int32),
            jax.ShapeDtypeStruct(table.shape, BF16),
        ),
        in_specs=[vmem] * 2,
        out_specs=(vmem,) * 2,
        compiler_params=params,
        name="ask_rows",
    )(jnp.transpose(requests), table)
    asked = lax.all_to_all(
        asks.reshape(ranges, 1, 128), "range", split_axis=0, concat_axis=0, tiled=True
    )
    picked = pl.pallas_call(
        pick_kernel,
        out_shape=jax.ShapeDtypeStruct((ranges * cap, width), BF16),
        in_specs=[vmem] * 2,
        out_specs=vmem,
        compiler_params=params,
        name="pick_rows",
    )(asked.reshape(ranges, 128), held)
    buffer = lax.all_to_all(
        picked.reshape(ranges, cap, width), "range", split_axis=0, concat_axis=0, tiled=True
    ).reshape(ranges * cap, width)

    smem = pl.BlockSpec(memory_space=pltpu.SMEM)
    anywhere = pl.BlockSpec(memory_space=pl.ANY)
    keep, send, moved = pl.pallas_call(
        functools.partial(step_kernel, float(length * ranges * tiles), share),
        out_shape=(
            jax.ShapeDtypeStruct((half, 128), BF16),
            jax.ShapeDtypeStruct((half, 128), BF16),
            jax.ShapeDtypeStruct((2 * length, 128), BF16),
        ),
        in_specs=[smem] + [vmem] * 13,
        out_specs=(anywhere, anywhere, vmem),
        scratch_shapes=[
            pltpu.VMEM((8, length), jnp.int32),
            pltpu.VMEM((2, half, 128), BF16),
            pltpu.VMEM((16, 128), F32),
            pltpu.VMEM((HEADS, length, length), F32),
            pltpu.SemaphoreType.DMA((2,)),
        ],
        compiler_params=params,
        name="window_step",
    )(
        core,
        features,
        buffer,
        jnp.transpose(ctx_slot[0]),
        labels,
        relay_slot,
        w_ctx,
        w_query,
        w_key,
        w_value,
        w_proj,
        w_logit,
        gain_attn.reshape(1, width),
        gain_out.reshape(1, width),
    )

    def exchange(lines, axis, groups=None):
        return lax.all_to_all(
            lines, axis, split_axis=0, concat_axis=0, tiled=True, axis_index_groups=groups
        )

    def total(parts):
        return lax.optimization_barrier(jnp.sum(parts.astype(F32), axis=0)).astype(BF16)

    def at(y, z, c):
        return (y * side + z) * 2 + c

    sides = range(side)
    swap = [(i, i ^ 1) for i in range(ranges)]
    along_z = [[at(y, z, c) for z in sides] for y in sides for c in range(2)]
    along_y = [[at(y, z, c) for y in sides] for z in sides for c in range(2)]

    other = lax.ppermute(send, "range", swap)
    pair = (keep.astype(F32) + other.astype(F32)).astype(BF16)
    part = total(exchange(pair.reshape(tiles, quarter, 128), "dp"))
    piece = total(exchange(part.reshape(side, piece_rows, 128), "range", along_z))

    def with_rows(lines, rows):
        repeated = jnp.broadcast_to(lines[None], (side, piece_rows, 128))
        return jnp.concatenate([repeated, rows.reshape(side, moved_rows, 128)], axis=1)

    parts = exchange(with_rows(piece, moved), "range", along_y)
    piece = total(parts[:, :piece_rows])
    moved = parts[:, piece_rows:].reshape(side, side, moved_rows // side, 128).swapaxes(0, 1)
    parts = exchange(with_rows(piece, moved), "range", along_z)
    own_rows = parts[:, piece_rows:].reshape(2 * length, 128)
    part = jnp.broadcast_to(parts[:, :piece_rows].reshape(1, quarter, 128), (tiles, quarter, 128))
    own = exchange(part, "dp").reshape(half, 128)
    other = lax.ppermute(jnp.concatenate([own, own_rows], axis=0), "range", swap)

    square = jax.ShapeDtypeStruct((width, width), F32)
    line = jax.ShapeDtypeStruct((1, width), F32)
    outs = pl.pallas_call(
        functools.partial(unpack_kernel, share, side),
        out_shape=(
            jax.ShapeDtypeStruct((length, width), BF16),
            jax.ShapeDtypeStruct(w_ctx.shape, F32),
        )
        + (square,) * 5
        + (line, line, jax.ShapeDtypeStruct((1, 1), F32)),
        in_specs=[smem] + [vmem] * 3,
        out_specs=(vmem,) * 10,
        compiler_params=params,
        name="unpack",
    )(core, own, own_rows, other)
    return (
        outs[0][None],
        outs[9].reshape(()),
        outs[1],
        outs[2],
        outs[3],
        outs[4],
        outs[5],
        outs[6],
        outs[7].reshape(width),
        outs[8].reshape(width),
    )


def solution(mesh):
    placed = (
        P("dp", "range", None),
        P("dp", "range", None),
        P("dp", "range", None, None),
        P("dp", "range", None),
        P("dp", "range"),
        P("dp", "range"),
        P(),
        P(),
        P(),
        P(),
        P(),
        P(),
        P(),
        P(),
    )
    return jax.shard_map(
        body,
        mesh=mesh,
        in_specs=placed,
        out_specs=(P("dp", "range", None), P(), P(), P(), P(), P(), P(), P(), P(), P()),
        check_vma=False,
    )
```

```python
import functools

import jax
import jax.numpy as jnp
from jax import lax
from jax.experimental import pallas as pl
from jax.experimental.pallas import tpu as pltpu
from jax.sharding import PartitionSpec as P

HEADS = 4
RANGE = ("chip", "core")
F32 = jnp.float32
BF16 = jnp.bfloat16


def nn(a, b):
    return lax.dot_general(a, b, (((1,), (0,)), ((), ())), preferred_element_type=F32)


def nt(a, b):
    return lax.dot_general(a, b, (((1,), (1,)), ((), ())), preferred_element_type=F32)


def tn(a, b):
    return lax.dot_general(a, b, (((0,), (0,)), ((), ())), preferred_element_type=F32)


def ask_kernel(asks_ref, table_ref, out_ref, held_ref):
    cap, owners = asks_ref.shape
    lines = jnp.concatenate([asks_ref[...], jnp.zeros((128 - cap, owners), jnp.int32)], axis=0)
    out_ref[...] = jnp.transpose(lines)
    held_ref[...] = table_ref[...]


def pick_kernel(idx_ref, table_ref, out_ref):
    asks, lanes = idx_ref.shape
    rows = out_ref.shape[0]
    cap = rows // asks
    table_rows = table_ref.shape[0]
    line = lax.broadcasted_iota(jnp.int32, (rows, asks), 0)
    spread = (line // cap == lax.broadcasted_iota(jnp.int32, (rows, asks), 1)).astype(BF16)
    ids = nn(spread, idx_ref[...].astype(F32).astype(BF16))
    own = lax.broadcasted_iota(jnp.int32, (rows, lanes), 0) % cap == lax.broadcasted_iota(
        jnp.int32, (rows, lanes), 1
    )
    ids = jnp.sum(jnp.where(own, ids, 0.0), axis=1, keepdims=True).astype(jnp.int32)
    hot = (ids == lax.broadcasted_iota(jnp.int32, (rows, table_rows), 1)).astype(BF16)
    out_ref[...] = nn(hot, table_ref[...]).astype(BF16)


def step_kernel(
    node_total,
    share,
    core_ref,
    feats_ref,
    buf_ref,
    slot_ref,
    label_ref,
    relay_ref,
    w_ctx_ref,
    w_query_ref,
    w_key_ref,
    w_value_ref,
    w_proj_ref,
    w_logit_ref,
    gain_attn_ref,
    gain_out_ref,
    keep_ref,
    send_ref,
    relayed_ref,
    ids_ref,
    slab_ref,
    extra_ref,
    prob_ref,
    sems,
):
    length, width = feats_ref.shape
    slots = buf_ref.shape[0]
    kc = slot_ref.shape[0]
    head_width = width // HEADS

    ids_ref[0:kc, :] = slot_ref[...]
    ids_ref[kc : kc + 1, :] = label_ref[...]
    ids_ref[kc + 1 :, :] = jnp.zeros((8 - kc - 1, length), jnp.int32)
    ids = jnp.transpose(ids_ref[...])

    buf = buf_ref[...]
    slot_lane = lax.broadcasted_iota(jnp.int32, (length, slots), 1)
    contexts = []
    hidden0 = feats_ref[...].astype(F32)
    for k in range(kc):
        hot = (ids[:, k : k + 1] == slot_lane).astype(BF16)
        part = nn(hot, buf).astype(BF16)
        contexts.append(part)
        hidden0 = hidden0 + nn(part, w_ctx_ref[k * width : (k + 1) * width, :])

    gain_attn = gain_attn_ref[...]
    inv1 = lax.rsqrt(jnp.mean(hidden0 * hidden0, axis=1, keepdims=True) + 1e-06)
    unit1 = hidden0 * inv1
    normed = (unit1 * gain_attn).astype(BF16)
    queries = nn(normed, w_query_ref[...]).astype(BF16)
    key_rows = nn(normed, w_key_ref[...]).astype(BF16)
    value_rows = nn(normed, w_value_ref[...]).astype(BF16)

    lane_head = lax.broadcasted_iota(jnp.int32, (length, width), 1) // head_width
    causal = lax.broadcasted_iota(jnp.int32, (length, length), 0) >= lax.broadcasted_iota(
        jnp.int32, (length, length), 1
    )
    scale = 1.0 / head_width**0.5

    def of_head(rows, h):
        return jnp.where(lane_head == h, rows, jnp.zeros_like(rows))

    attended = jnp.zeros((length, width), F32)
    for h in range(HEADS):
        scores = nt(of_head(queries, h), key_rows) * scale
        scores = jnp.where(causal, scores, -1e30)
        expo = jnp.exp(scores - jnp.max(scores, axis=1, keepdims=True))
        prob = expo / jnp.sum(expo, axis=1, keepdims=True)
        prob_ref[h] = prob
        attended = attended + nn(prob.astype(BF16), of_head(value_rows, h))
    attended = attended.astype(BF16)
    hidden1 = hidden0 + nn(attended, w_proj_ref[...])

    line = lax.broadcasted_iota(jnp.int32, (2 * length, length), 0)
    place = relay_ref[...] == line // (2 * share) * share + line % share
    moved = nn(place.astype(BF16), hidden1.astype(BF16))
    line = lax.broadcasted_iota(jnp.int32, (2 * length, 128), 0)
    left = line // share % 2 == 0
    relayed_ref[...] = jnp.where(left, moved[:, :128], moved[:, 128:]).astype(BF16)

    gain_out = gain_out_ref[...]
    inv2 = lax.rsqrt(jnp.mean(hidden1 * hidden1, axis=1, keepdims=True) + 1e-06)
    unit2 = hidden1 * inv2
    normed_out = (unit2 * gain_out).astype(BF16)
    logits = nn(normed_out, w_logit_ref[...])
    symbol = lax.broadcasted_iota(jnp.int32, logits.shape, 1)
    target = symbol == ids[:, kc : kc + 1]
    logit_max = jnp.max(logits, axis=1, keepdims=True)
    expo = jnp.exp(logits - logit_max)
    total = jnp.sum(expo, axis=1, keepdims=True)
    picked = jnp.sum(jnp.where(target, logits, 0.0), axis=1, keepdims=True)
    losses = logit_max + jnp.log(total) - picked
    lane = lax.broadcasted_iota(jnp.int32, (length, 128), 1)
    own_lane = lax.broadcasted_iota(jnp.int32, (length, 128), 0) % 128 == lane
    loss = jnp.sum(jnp.where(own_lane, losses, 0.0), axis=0, keepdims=True) * (1.0 / node_total)

    g_logits = ((expo / total - target.astype(F32)) * (1.0 / node_total)).astype(BF16)
    g_w_logit = tn(normed_out, g_logits).astype(BF16)
    g_normed_out = nt(g_logits, w_logit_ref[...]).astype(BF16).astype(F32)
    g_gain_out = jnp.sum(g_normed_out * unit2, axis=0, keepdims=True)
    g_unit = g_normed_out * gain_out
    g_hidden1 = inv2 * (g_unit - unit2 * jnp.mean(g_unit * unit2, axis=1, keepdims=True))
    g_rows = g_hidden1.astype(BF16)
    g_w_proj = tn(attended, g_rows).astype(BF16)
    g_attended = nt(g_rows, w_proj_ref[...]).astype(BF16)

    g_queries = jnp.zeros((length, width), F32)
    g_keys = jnp.zeros((length, width), F32)
    g_values = jnp.zeros((length, width), F32)
    for h in range(HEADS):
        prob = prob_ref[h]
        g_att_h = of_head(g_attended, h)
        g_prob = nt(g_att_h, value_rows).astype(BF16).astype(F32)
        g_values = g_values + tn(prob.astype(BF16), g_att_h)
        weighed = jnp.sum(g_prob * prob, axis=1, keepdims=True)
        g_scores = (prob * (g_prob - weighed) * scale).astype(BF16)
        g_queries = g_queries + nn(g_scores, of_head(key_rows, h))
        g_keys = g_keys + tn(g_scores, of_head(queries, h))
    g_queries = g_queries.astype(BF16)
    g_keys = g_keys.astype(BF16)
    g_values = g_values.astype(BF16)
    g_w_query = tn(normed, g_queries).astype(BF16)
    g_w_key = tn(normed, g_keys).astype(BF16)
    g_w_value = tn(normed, g_values).astype(BF16)
    g_normed = (
        nt(g_queries, w_query_ref[...])
        + nt(g_keys, w_key_ref[...])
        + nt(g_values, w_value_ref[...])
    )
    g_gain_attn = jnp.sum(g_normed * unit1, axis=0, keepdims=True)
    g_unit = g_normed * gain_attn
    g_hidden0 = g_hidden1 + inv1 * (
        g_unit - unit1 * jnp.mean(g_unit * unit1, axis=1, keepdims=True)
    )
    g_rows = g_hidden0.astype(BF16)
    for k in range(kc):
        g_w_ctx = tn(contexts[k], g_rows).astype(BF16)
        slab_ref[0, k * width : (k + 1) * width, :] = g_w_ctx[:, :128]
        slab_ref[0, (kc + k) * width : (kc + k + 1) * width, :] = g_w_ctx[:, 128:]
    first = 2 * kc * width
    slab_ref[0, first : first + width, :] = g_w_logit[:, :128]
    slab_ref[1, 0:width, :] = g_w_logit[:, 128:]
    row = width
    for grad in (g_w_query, g_w_key, g_w_value, g_w_proj):
        slab_ref[1, row : row + width, :] = grad[:, :128]
        slab_ref[1, row + width : row + 2 * width, :] = grad[:, 128:]
        row += 2 * width
    extra_ref[...] = jnp.zeros_like(extra_ref)
    extra_ref[0:1, :] = g_gain_attn[:, :128]
    extra_ref[1:2, :] = g_gain_attn[:, 128:]
    extra_ref[2:3, :] = g_gain_out[:, :128]
    extra_ref[3:4, :] = g_gain_out[:, 128:]
    extra_ref[4:5, :] = loss
    used = first + width
    slab_ref[0, used : used + 16, :] = extra_ref[...].astype(BF16)
    half = slab_ref.shape[1]
    slab_ref[0, used + 16 :, :] = jnp.zeros((half - used - 16, 128), BF16)
    slab_ref[1, used:, :] = jnp.zeros((half - used, 128), BF16)

    core = core_ref[0]
    keep = pltpu.make_async_copy(slab_ref.at[core], keep_ref, sems.at[0])
    send = pltpu.make_async_copy(slab_ref.at[1 - core], send_ref, sems.at[1])
    keep.start()
    send.start()
    keep.wait()
    send.wait()


def unpack_kernel(
    share,
    core_ref,
    own_ref,
    own_rows_ref,
    other_ref,
    relayed_ref,
    ctx_ref,
    query_ref,
    key_ref,
    value_ref,
    proj_ref,
    logit_ref,
    attn_ref,
    out_ref,
    loss_ref,
):
    core = core_ref[0]
    rows = ctx_ref.shape[0]
    width = logit_ref.shape[0]
    half = own_ref.shape[0]

    def lines(h, start, count):
        mine = own_ref[start : start + count, :].astype(F32)
        theirs = other_ref[start : start + count, :].astype(F32)
        return jnp.where(core == h, mine, theirs)

    for row in range(0, rows, width):
        ctx_ref[row : row + width, :128] = lines(0, row, width)
        ctx_ref[row : row + width, 128:] = lines(0, rows + row, width)
    logit_ref[:, :128] = lines(0, 2 * rows, width)
    logit_ref[:, 128:] = lines(1, 0, width)
    row = width
    for ref in (query_ref, key_ref, value_ref, proj_ref):
        ref[:, :128] = lines(1, row, width)
        ref[:, 128:] = lines(1, row + width, width)
        row += 2 * width
    extra = lines(0, 2 * rows + width, 16)
    attn_ref[:, :128] = extra[0:1]
    attn_ref[:, 128:] = extra[1:2]
    out_ref[:, :128] = extra[2:3]
    out_ref[:, 128:] = extra[3:4]
    loss_ref[...] = jnp.sum(extra[4:5], axis=1, keepdims=True)

    length = relayed_ref.shape[0]
    row = lax.broadcasted_iota(jnp.int32, (length, 2 * length), 0)
    line = lax.broadcasted_iota(jnp.int32, (length, 2 * length), 1)
    mine = row // share % 2 == core
    own_rows = own_rows_ref[...]
    other_rows = other_ref[half:, :]
    for h in range(2):
        found = line == (row // (2 * share) * 4 + 2 * core + h) * share + row % share
        here = (found & mine).astype(BF16)
        there = (found & ~mine).astype(BF16)
        relayed_ref[:, h * 128 : (h + 1) * 128] = (
            nn(here, own_rows) + nn(there, other_rows)
        ).astype(BF16)


def body(
    node_feats,
    ctx_table,
    fetch_rows,
    ctx_slot,
    labels,
    relay_slot,
    w_ctx,
    w_query,
    w_key,
    w_value,
    w_proj,
    w_logit,
    gain_attn,
    gain_out,
):
    features = node_feats[0]
    length, width = features.shape
    chips, ranges = lax.axis_size("chip"), lax.axis_size(RANGE)
    table = ctx_table[0]
    requests = fetch_rows[0, 0]
    cap = requests.shape[1]
    tiles = lax.axis_size("dp")
    share = length // ranges
    core = lax.axis_index("core").astype(jnp.int32).reshape(1)
    half = (w_ctx.shape[0] * width + 5 * width * width) // 256 + 16
    half = -(-half // (2 * tiles * chips)) * (2 * tiles * chips)
    quarter = half // tiles
    pairs = quarter // (2 * chips)
    moved_pairs = length // chips
    vmem = pl.BlockSpec(memory_space=pltpu.VMEM)
    params = pltpu.CompilerParams(vmem_limit_bytes=32 * 1024 * 1024)

    asks, held = pl.pallas_call(
        ask_kernel,
        out_shape=(
            jax.ShapeDtypeStruct((ranges, 128), jnp.int32),
            jax.ShapeDtypeStruct(table.shape, BF16),
        ),
        in_specs=[vmem] * 2,
        out_specs=(vmem,) * 2,
        compiler_params=params,
        name="ask_rows",
    )(jnp.transpose(requests), table)
    asked = lax.all_to_all(
        asks.reshape(ranges, 1, 128), RANGE, split_axis=0, concat_axis=0, tiled=True
    )
    picked = pl.pallas_call(
        pick_kernel,
        out_shape=jax.ShapeDtypeStruct((ranges * cap, width), BF16),
        in_specs=[vmem] * 2,
        out_specs=vmem,
        compiler_params=params,
        name="pick_rows",
    )(asked.reshape(ranges, 128), held)
    buffer = lax.all_to_all(
        picked.reshape(ranges, cap, width), RANGE, split_axis=0, concat_axis=0, tiled=True
    ).reshape(ranges * cap, width)

    smem = pl.BlockSpec(memory_space=pltpu.SMEM)
    anywhere = pl.BlockSpec(memory_space=pl.ANY)
    keep, send, moved = pl.pallas_call(
        functools.partial(step_kernel, float(length * ranges * tiles), share),
        out_shape=(
            jax.ShapeDtypeStruct((half, 128), BF16),
            jax.ShapeDtypeStruct((half, 128), BF16),
            jax.ShapeDtypeStruct((2 * length, 128), BF16),
        ),
        in_specs=[smem] + [vmem] * 13,
        out_specs=(anywhere, anywhere, vmem),
        scratch_shapes=[
            pltpu.VMEM((8, length), jnp.int32),
            pltpu.VMEM((2, half, 128), BF16),
            pltpu.VMEM((16, 128), F32),
            pltpu.VMEM((HEADS, length, length), F32),
            pltpu.SemaphoreType.DMA((2,)),
        ],
        compiler_params=params,
        name="window_step",
    )(
        core,
        features,
        buffer,
        jnp.transpose(ctx_slot[0]),
        labels,
        relay_slot,
        w_ctx,
        w_query,
        w_key,
        w_value,
        w_proj,
        w_logit,
        gain_attn.reshape(1, width),
        gain_out.reshape(1, width),
    )

    def exchange(lines, axis):
        return lax.all_to_all(lines, axis, split_axis=0, concat_axis=0, tiled=True)

    def total(parts):
        return lax.optimization_barrier(jnp.sum(parts.astype(F32), axis=0)).astype(BF16)

    swap = [(0, 1), (1, 0)]
    other = lax.ppermute(send, "core", swap)
    pair = (keep.astype(F32) + other.astype(F32)).astype(BF16)
    part = total(exchange(pair.reshape(tiles, quarter, 128), "dp"))
    piece = total(exchange(part.reshape(chips, pairs, 2, 128), "chip"))

    repeated = jnp.broadcast_to(piece[None], (chips, pairs, 2, 128))
    moved = moved.reshape(chips, moved_pairs, 2, 128)
    parts = exchange(jnp.concatenate([repeated, moved], axis=1), "chip")
    own_rows = parts[:, pairs:].reshape(2 * length, 128)
    part = jnp.broadcast_to(parts[:, :pairs].reshape(1, quarter, 128), (tiles, quarter, 128))
    own = exchange(part, "dp").reshape(half, 128)
    other = lax.ppermute(jnp.concatenate([own, own_rows], axis=0), "core", swap)

    square = jax.ShapeDtypeStruct((width, width), F32)
    line = jax.ShapeDtypeStruct((1, width), F32)
    outs = pl.pallas_call(
        functools.partial(unpack_kernel, share),
        out_shape=(
            jax.ShapeDtypeStruct((length, width), BF16),
            jax.ShapeDtypeStruct(w_ctx.shape, F32),
        )
        + (square,) * 5
        + (line, line, jax.ShapeDtypeStruct((1, 1), F32)),
        in_specs=[smem] + [vmem] * 3,
        out_specs=(vmem,) * 10,
        compiler_params=params,
        name="unpack",
    )(core, own, own_rows, other)
    return (
        outs[0][None],
        outs[9].reshape(()),
        outs[1],
        outs[2],
        outs[3],
        outs[4],
        outs[5],
        outs[6],
        outs[7].reshape(width),
        outs[8].reshape(width),
    )


def solution(mesh):
    ranges, tiles = mesh.devices.shape
    split = jax.sharding.Mesh(
        mesh.devices.reshape(ranges // 2, 2, tiles), ("chip", "core", "dp")
    )
    placed = (
        P("dp", RANGE, None),
        P("dp", RANGE, None),
        P("dp", RANGE, None, None),
        P("dp", RANGE, None),
        P("dp", RANGE),
        P("dp", RANGE),
        P(),
        P(),
        P(),
        P(),
        P(),
        P(),
        P(),
        P(),
    )
    return jax.shard_map(
        body,
        mesh=split,
        in_specs=placed,
        out_specs=(P("dp", RANGE, None), P(), P(), P(), P(), P(), P(), P(), P(), P()),
        check_vma=False,
    )
```

```python
import functools

import jax
import jax.numpy as jnp
from jax import lax
from jax.experimental import pallas as pl
from jax.experimental.pallas import tpu as pltpu
from jax.sharding import PartitionSpec as P

HEADS = 4
RANGE = ("chip", "core")
F32 = jnp.float32
BF16 = jnp.bfloat16


def nn(a, b):
    return lax.dot_general(a, b, (((1,), (0,)), ((), ())), preferred_element_type=F32)


def nt(a, b):
    return lax.dot_general(a, b, (((1,), (1,)), ((), ())), preferred_element_type=F32)


def tn(a, b):
    return lax.dot_general(a, b, (((0,), (0,)), ((), ())), preferred_element_type=F32)


def ask_kernel(asks_ref, table_ref, out_ref, held_ref, lines_ref, sems):
    cap = asks_ref.shape[0]
    asks = pltpu.make_async_copy(asks_ref, lines_ref.at[0:cap, :], sems.at[0])
    table = pltpu.make_async_copy(table_ref, held_ref, sems.at[1])
    asks.start()
    table.start()
    lines_ref[cap:, :] = jnp.zeros((lines_ref.shape[0] - cap, lines_ref.shape[1]), jnp.int32)
    asks.wait()
    out_ref[...] = jnp.transpose(lines_ref[...])
    table.wait()


def pick_kernel(core_ref, idx_ref, own_ref, other_ref, out_ref):
    asks, lanes = idx_ref.shape
    rows = out_ref.shape[0]
    cap = rows // asks
    line = lax.broadcasted_iota(jnp.int32, (rows, asks), 0)
    spread = (line // cap == lax.broadcasted_iota(jnp.int32, (rows, asks), 1)).astype(BF16)
    ids = nn(spread, idx_ref[...].astype(F32).astype(BF16))
    own = lax.broadcasted_iota(jnp.int32, (rows, lanes), 0) % cap == lax.broadcasted_iota(
        jnp.int32, (rows, lanes), 1
    )
    ids = jnp.sum(jnp.where(own, ids, 0.0), axis=1, keepdims=True).astype(jnp.int32)
    hot = ids == lax.broadcasted_iota(jnp.int32, (rows, own_ref.shape[0]), 1)
    mine = lax.broadcasted_iota(jnp.int32, hot.shape, 0) // cap % 2 == core_ref[0]
    out_ref[...] = (
        nn((hot & mine).astype(BF16), own_ref[...])
        + nn((hot & ~mine).astype(BF16), other_ref[...])
    ).astype(BF16)


def step_kernel(
    node_total,
    share,
    core_ref,
    feats_ref,
    buf_ref,
    slot_ref,
    label_ref,
    relay_ref,
    w_ctx_ref,
    w_query_ref,
    w_key_ref,
    w_value_ref,
    w_proj_ref,
    w_logit_ref,
    gain_attn_ref,
    gain_out_ref,
    keep_ref,
    send_ref,
    relayed_ref,
    ids_ref,
    slab_ref,
    extra_ref,
    prob_ref,
    sems,
):
    length, width = feats_ref.shape
    slots = buf_ref.shape[0]
    kc = slot_ref.shape[0]
    head_width = width // HEADS

    ids_ref[0:kc, :] = slot_ref[...]
    ids_ref[kc : kc + 1, :] = label_ref[...]
    ids_ref[kc + 1 :, :] = jnp.zeros((8 - kc - 1, length), jnp.int32)
    ids = jnp.transpose(ids_ref[...])

    buf = buf_ref[...]
    slot_lane = lax.broadcasted_iota(jnp.int32, (length, slots), 1)
    contexts = []
    hidden0 = feats_ref[...].astype(F32)
    for k in range(kc):
        hot = (ids[:, k : k + 1] == slot_lane).astype(BF16)
        part = nn(hot, buf).astype(BF16)
        contexts.append(part)
        hidden0 = hidden0 + nn(part, w_ctx_ref[k * width : (k + 1) * width, :])

    gain_attn = gain_attn_ref[...]
    inv1 = lax.rsqrt(jnp.mean(hidden0 * hidden0, axis=1, keepdims=True) + 1e-06)
    unit1 = hidden0 * inv1
    normed = (unit1 * gain_attn).astype(BF16)
    queries = nn(normed, w_query_ref[...]).astype(BF16)
    key_rows = nn(normed, w_key_ref[...]).astype(BF16)
    value_rows = nn(normed, w_value_ref[...]).astype(BF16)

    lane_head = lax.broadcasted_iota(jnp.int32, (length, width), 1) // head_width
    causal = lax.broadcasted_iota(jnp.int32, (length, length), 0) >= lax.broadcasted_iota(
        jnp.int32, (length, length), 1
    )
    scale = 1.0 / head_width**0.5

    def of_head(rows, h):
        return jnp.where(lane_head == h, rows, jnp.zeros_like(rows))

    attended = jnp.zeros((length, width), F32)
    for h in range(HEADS):
        scores = nt(of_head(queries, h), key_rows) * scale
        scores = jnp.where(causal, scores, -1e30)
        expo = jnp.exp(scores - jnp.max(scores, axis=1, keepdims=True))
        prob = expo / jnp.sum(expo, axis=1, keepdims=True)
        prob_ref[h] = prob
        attended = attended + nn(prob.astype(BF16), of_head(value_rows, h))
    attended = attended.astype(BF16)
    hidden1 = hidden0 + nn(attended, w_proj_ref[...])

    line = lax.broadcasted_iota(jnp.int32, (2 * length, length), 0)
    place = relay_ref[...] == line // (2 * share) * share + line % share
    moved = nn(place.astype(BF16), hidden1.astype(BF16))
    line = lax.broadcasted_iota(jnp.int32, (2 * length, 128), 0)
    left = line // share % 2 == 0
    relayed_ref[...] = jnp.where(left, moved[:, :128], moved[:, 128:]).astype(BF16)

    gain_out = gain_out_ref[...]
    inv2 = lax.rsqrt(jnp.mean(hidden1 * hidden1, axis=1, keepdims=True) + 1e-06)
    unit2 = hidden1 * inv2
    normed_out = (unit2 * gain_out).astype(BF16)
    logits = nn(normed_out, w_logit_ref[...])
    symbol = lax.broadcasted_iota(jnp.int32, logits.shape, 1)
    target = symbol == ids[:, kc : kc + 1]
    logit_max = jnp.max(logits, axis=1, keepdims=True)
    expo = jnp.exp(logits - logit_max)
    total = jnp.sum(expo, axis=1, keepdims=True)
    picked = jnp.sum(jnp.where(target, logits, 0.0), axis=1, keepdims=True)
    losses = logit_max + jnp.log(total) - picked
    lane = lax.broadcasted_iota(jnp.int32, (length, 128), 1)
    own_lane = lax.broadcasted_iota(jnp.int32, (length, 128), 0) % 128 == lane
    loss = jnp.sum(jnp.where(own_lane, losses, 0.0), axis=0, keepdims=True) * (1.0 / node_total)

    g_logits = ((expo / total - target.astype(F32)) * (1.0 / node_total)).astype(BF16)
    g_w_logit = tn(normed_out, g_logits).astype(BF16)
    g_normed_out = nt(g_logits, w_logit_ref[...]).astype(BF16).astype(F32)
    g_gain_out = jnp.sum(g_normed_out * unit2, axis=0, keepdims=True)
    g_unit = g_normed_out * gain_out
    g_hidden1 = inv2 * (g_unit - unit2 * jnp.mean(g_unit * unit2, axis=1, keepdims=True))
    g_rows = g_hidden1.astype(BF16)
    g_w_proj = tn(attended, g_rows).astype(BF16)
    g_attended = nt(g_rows, w_proj_ref[...]).astype(BF16)

    g_queries = jnp.zeros((length, width), F32)
    g_keys = jnp.zeros((length, width), F32)
    g_values = jnp.zeros((length, width), F32)
    for h in range(HEADS):
        prob = prob_ref[h]
        g_att_h = of_head(g_attended, h)
        g_prob = nt(g_att_h, value_rows).astype(BF16).astype(F32)
        g_values = g_values + tn(prob.astype(BF16), g_att_h)
        weighed = jnp.sum(g_prob * prob, axis=1, keepdims=True)
        g_scores = (prob * (g_prob - weighed) * scale).astype(BF16)
        g_queries = g_queries + nn(g_scores, of_head(key_rows, h))
        g_keys = g_keys + tn(g_scores, of_head(queries, h))
    g_queries = g_queries.astype(BF16)
    g_keys = g_keys.astype(BF16)
    g_values = g_values.astype(BF16)
    g_w_query = tn(normed, g_queries).astype(BF16)
    g_w_key = tn(normed, g_keys).astype(BF16)
    g_w_value = tn(normed, g_values).astype(BF16)
    g_normed = (
        nt(g_queries, w_query_ref[...])
        + nt(g_keys, w_key_ref[...])
        + nt(g_values, w_value_ref[...])
    )
    g_gain_attn = jnp.sum(g_normed * unit1, axis=0, keepdims=True)
    g_unit = g_normed * gain_attn
    g_hidden0 = g_hidden1 + inv1 * (
        g_unit - unit1 * jnp.mean(g_unit * unit1, axis=1, keepdims=True)
    )
    g_rows = g_hidden0.astype(BF16)
    for k in range(kc):
        g_w_ctx = tn(contexts[k], g_rows).astype(BF16)
        slab_ref[0, k * width : (k + 1) * width, :] = g_w_ctx[:, :128]
        slab_ref[0, (kc + k) * width : (kc + k + 1) * width, :] = g_w_ctx[:, 128:]
    first = 2 * kc * width
    slab_ref[0, first : first + width, :] = g_w_logit[:, :128]
    slab_ref[1, 0:width, :] = g_w_logit[:, 128:]
    row = width
    for grad in (g_w_query, g_w_key, g_w_value, g_w_proj):
        slab_ref[1, row : row + width, :] = grad[:, :128]
        slab_ref[1, row + width : row + 2 * width, :] = grad[:, 128:]
        row += 2 * width
    extra_ref[...] = jnp.zeros_like(extra_ref)
    extra_ref[0:1, :] = g_gain_attn[:, :128]
    extra_ref[1:2, :] = g_gain_attn[:, 128:]
    extra_ref[2:3, :] = g_gain_out[:, :128]
    extra_ref[3:4, :] = g_gain_out[:, 128:]
    extra_ref[4:5, :] = loss
    used = first + width
    slab_ref[0, used : used + 16, :] = extra_ref[...].astype(BF16)
    half = slab_ref.shape[1]
    slab_ref[0, used + 16 :, :] = jnp.zeros((half - used - 16, 128), BF16)
    slab_ref[1, used:, :] = jnp.zeros((half - used, 128), BF16)

    core = core_ref[0]
    keep = pltpu.make_async_copy(slab_ref.at[core], keep_ref, sems.at[0])
    send = pltpu.make_async_copy(slab_ref.at[1 - core], send_ref, sems.at[1])
    keep.start()
    send.start()
    keep.wait()
    send.wait()


def unpack_kernel(
    share,
    core_ref,
    own_ref,
    own_rows_ref,
    other_ref,
    relayed_ref,
    ctx_ref,
    query_ref,
    key_ref,
    value_ref,
    proj_ref,
    logit_ref,
    attn_ref,
    out_ref,
    loss_ref,
):
    core = core_ref[0]
    rows = ctx_ref.shape[0]
    width = logit_ref.shape[0]
    half = own_ref.shape[0]

    def lines(h, start, count):
        mine = own_ref[start : start + count, :].astype(F32)
        theirs = other_ref[start : start + count, :].astype(F32)
        return jnp.where(core == h, mine, theirs)

    for row in range(0, rows, width):
        ctx_ref[row : row + width, :128] = lines(0, row, width)
        ctx_ref[row : row + width, 128:] = lines(0, rows + row, width)
    logit_ref[:, :128] = lines(0, 2 * rows, width)
    logit_ref[:, 128:] = lines(1, 0, width)
    row = width
    for ref in (query_ref, key_ref, value_ref, proj_ref):
        ref[:, :128] = lines(1, row, width)
        ref[:, 128:] = lines(1, row + width, width)
        row += 2 * width
    extra = lines(0, 2 * rows + width, 16)
    attn_ref[:, :128] = extra[0:1]
    attn_ref[:, 128:] = extra[1:2]
    out_ref[:, :128] = extra[2:3]
    out_ref[:, 128:] = extra[3:4]
    loss_ref[...] = jnp.sum(extra[4:5], axis=1, keepdims=True)

    length = relayed_ref.shape[0]
    row = lax.broadcasted_iota(jnp.int32, (length, 2 * length), 0)
    line = lax.broadcasted_iota(jnp.int32, (length, 2 * length), 1)
    mine = row // share % 2 == core
    own_rows = own_rows_ref[...]
    other_rows = other_ref[half:, :]
    for h in range(2):
        found = line == (row // (2 * share) * 4 + 2 * core + h) * share + row % share
        here = (found & mine).astype(BF16)
        there = (found & ~mine).astype(BF16)
        relayed_ref[:, h * 128 : (h + 1) * 128] = (
            nn(here, own_rows) + nn(there, other_rows)
        ).astype(BF16)


def body(
    node_feats,
    ctx_table,
    fetch_rows,
    ctx_slot,
    labels,
    relay_slot,
    w_ctx,
    w_query,
    w_key,
    w_value,
    w_proj,
    w_logit,
    gain_attn,
    gain_out,
):
    features = node_feats[0]
    length, width = features.shape
    chips, ranges = lax.axis_size("chip"), lax.axis_size(RANGE)
    table = ctx_table[0]
    requests = fetch_rows[0, 0]
    cap = requests.shape[1]
    tiles = lax.axis_size("dp")
    share = length // ranges
    core = lax.axis_index("core").astype(jnp.int32).reshape(1)
    half = (w_ctx.shape[0] * width + 5 * width * width) // 256 + 16
    half = -(-half // (8 * chips)) * (8 * chips)
    piece_rows = half // chips
    moved_rows = 2 * length // chips
    swap = [(0, 1), (1, 0)]
    vmem = pl.BlockSpec(memory_space=pltpu.VMEM)
    params = pltpu.CompilerParams(vmem_limit_bytes=32 * 1024 * 1024)

    smem = pl.BlockSpec(memory_space=pltpu.SMEM)
    anywhere = pl.BlockSpec(memory_space=pl.ANY)

    def exchange(lines, axis):
        return lax.all_to_all(lines, axis, split_axis=0, concat_axis=0, tiled=True)

    asks, held = pl.pallas_call(
        ask_kernel,
        out_shape=(
            jax.ShapeDtypeStruct((ranges, 128), jnp.int32),
            jax.ShapeDtypeStruct(table.shape, BF16),
        ),
        in_specs=[pl.BlockSpec(memory_space=pltpu.HBM)] * 2,
        out_specs=(vmem,) * 2,
        scratch_shapes=[pltpu.VMEM((128, ranges), jnp.int32), pltpu.SemaphoreType.DMA((2,))],
        compiler_params=params,
        name="ask_rows",
    )(jnp.transpose(requests), table)
    asked = exchange(asks.reshape(chips, 2, 128), "chip")
    other_held = lax.ppermute(held, "core", swap)
    picked = pl.pallas_call(
        pick_kernel,
        out_shape=jax.ShapeDtypeStruct((ranges * cap, width), BF16),
        in_specs=[smem] + [vmem] * 3,
        out_specs=vmem,
        compiler_params=params,
        name="pick_rows",
    )(core, asked.reshape(ranges, 128), held, other_held)
    buffer = exchange(picked.reshape(chips, 2 * cap, width), "chip").reshape(ranges * cap, width)

    keep, send, moved = pl.pallas_call(
        functools.partial(step_kernel, float(length * ranges * tiles), share),
        out_shape=(
            jax.ShapeDtypeStruct((half, 128), BF16),
            jax.ShapeDtypeStruct((half, 128), BF16),
            jax.ShapeDtypeStruct((2 * length, 128), BF16),
        ),
        in_specs=[smem] + [vmem] * 13,
        out_specs=(anywhere, anywhere, vmem),
        scratch_shapes=[
            pltpu.VMEM((8, length), jnp.int32),
            pltpu.VMEM((2, half, 128), BF16),
            pltpu.VMEM((16, 128), F32),
            pltpu.VMEM((HEADS, length, length), F32),
            pltpu.SemaphoreType.DMA((2,)),
        ],
        compiler_params=params,
        name="window_step",
    )(
        core,
        features,
        buffer,
        jnp.transpose(ctx_slot[0]),
        labels,
        relay_slot,
        w_ctx,
        w_query,
        w_key,
        w_value,
        w_proj,
        w_logit,
        gain_attn.reshape(1, width),
        gain_out.reshape(1, width),
    )

    other = lax.ppermute(send, "core", swap)
    pair = (keep.astype(F32) + other.astype(F32)).astype(BF16)
    outgoing = [pair.reshape(chips, piece_rows, 128), moved.reshape(chips, moved_rows, 128)]
    parts = exchange(jnp.concatenate(outgoing, axis=1), "chip")
    own_rows = parts[:, piece_rows:].reshape(2 * length, 128)

    def total(parts):
        return lax.optimization_barrier(jnp.sum(parts.astype(F32), axis=0)).astype(BF16)

    piece = total(parts[:, :piece_rows])
    piece = total(exchange(jnp.broadcast_to(piece[None], (tiles, piece_rows, 128)), "dp"))
    own = exchange(jnp.broadcast_to(piece[None], (chips, piece_rows, 128)), "chip")
    own = own.reshape(half, 128)
    other = lax.ppermute(jnp.concatenate([own, own_rows], axis=0), "core", swap)

    square = jax.ShapeDtypeStruct((width, width), F32)
    line = jax.ShapeDtypeStruct((1, width), F32)
    outs = pl.pallas_call(
        functools.partial(unpack_kernel, share),
        out_shape=(
            jax.ShapeDtypeStruct((length, width), BF16),
            jax.ShapeDtypeStruct(w_ctx.shape, F32),
        )
        + (square,) * 5
        + (line, line, jax.ShapeDtypeStruct((1, 1), F32)),
        in_specs=[smem] + [vmem] * 3,
        out_specs=(vmem,) * 10,
        compiler_params=params,
        name="unpack",
    )(core, own, own_rows, other)
    return (
        outs[0][None],
        outs[9].reshape(()),
        outs[1],
        outs[2],
        outs[3],
        outs[4],
        outs[5],
        outs[6],
        outs[7].reshape(width),
        outs[8].reshape(width),
    )


def solution(mesh):
    ranges, tiles = mesh.devices.shape
    split = jax.sharding.Mesh(
        mesh.devices.reshape(ranges // 2, 2, tiles), ("chip", "core", "dp")
    )
    placed = (
        P("dp", RANGE, None),
        P("dp", RANGE, None),
        P("dp", RANGE, None, None),
        P("dp", RANGE, None),
        P("dp", RANGE),
        P("dp", RANGE),
        P(),
        P(),
        P(),
        P(),
        P(),
        P(),
        P(),
        P(),
    )
    return jax.shard_map(
        body,
        mesh=split,
        in_specs=placed,
        out_specs=(P("dp", RANGE, None), P(), P(), P(), P(), P(), P(), P(), P(), P()),
        check_vma=False,
    )
```

```python
import functools

import jax
import jax.numpy as jnp
from jax import lax
from jax.experimental import pallas as pl
from jax.experimental.pallas import tpu as pltpu
from jax.sharding import PartitionSpec as P

HEADS = 4
RANGE = ("chip", "core")
F32 = jnp.float32
BF16 = jnp.bfloat16


def nn(a, b):
    return lax.dot_general(a, b, (((1,), (0,)), ((), ())), preferred_element_type=F32)


def nt(a, b):
    return lax.dot_general(a, b, (((1,), (1,)), ((), ())), preferred_element_type=F32)


def tn(a, b):
    return lax.dot_general(a, b, (((0,), (0,)), ((), ())), preferred_element_type=F32)


def ask_kernel(asks_ref, table_ref, out_ref, held_ref):
    cap, owners = asks_ref.shape
    lines = jnp.concatenate([asks_ref[...], jnp.zeros((128 - cap, owners), jnp.int32)], axis=0)
    out_ref[...] = jnp.transpose(lines)
    held_ref[...] = table_ref[...]


def pick_kernel(core_ref, idx_ref, own_ref, other_ref, out_ref):
    asks, lanes = idx_ref.shape
    rows = out_ref.shape[0]
    cap = rows // asks
    line = lax.broadcasted_iota(jnp.int32, (rows, asks), 0)
    spread = (line // cap == lax.broadcasted_iota(jnp.int32, (rows, asks), 1)).astype(BF16)
    ids = nn(spread, idx_ref[...].astype(F32).astype(BF16))
    own = lax.broadcasted_iota(jnp.int32, (rows, lanes), 0) % cap == lax.broadcasted_iota(
        jnp.int32, (rows, lanes), 1
    )
    ids = jnp.sum(jnp.where(own, ids, 0.0), axis=1, keepdims=True).astype(jnp.int32)
    hot = ids == lax.broadcasted_iota(jnp.int32, (rows, own_ref.shape[0]), 1)
    mine = lax.broadcasted_iota(jnp.int32, hot.shape, 0) // cap % 2 == core_ref[0]
    out_ref[...] = (
        nn((hot & mine).astype(BF16), own_ref[...])
        + nn((hot & ~mine).astype(BF16), other_ref[...])
    ).astype(BF16)


def step_kernel(
    node_total,
    share,
    feats_ref,
    buf_ref,
    slot_ref,
    label_ref,
    relay_ref,
    w_ctx_ref,
    w_query_ref,
    w_key_ref,
    w_value_ref,
    w_proj_ref,
    w_logit_ref,
    gain_attn_ref,
    gain_out_ref,
    slab_ref,
    relayed_ref,
    ids_ref,
    extra_ref,
    prob_ref,
):
    length, width = feats_ref.shape
    slots = buf_ref.shape[0]
    kc = slot_ref.shape[0]
    head_width = width // HEADS

    ids_ref[0:kc, :] = slot_ref[...]
    ids_ref[kc : kc + 1, :] = label_ref[...]
    ids_ref[kc + 1 :, :] = jnp.zeros((8 - kc - 1, length), jnp.int32)
    ids = jnp.transpose(ids_ref[...])

    buf = buf_ref[...]
    slot_lane = lax.broadcasted_iota(jnp.int32, (length, slots), 1)
    contexts = []
    hidden0 = feats_ref[...].astype(F32)
    for k in range(kc):
        hot = (ids[:, k : k + 1] == slot_lane).astype(BF16)
        part = nn(hot, buf).astype(BF16)
        contexts.append(part)
        hidden0 = hidden0 + nn(part, w_ctx_ref[k * width : (k + 1) * width, :])

    gain_attn = gain_attn_ref[...]
    inv1 = lax.rsqrt(jnp.mean(hidden0 * hidden0, axis=1, keepdims=True) + 1e-06)
    unit1 = hidden0 * inv1
    normed = (unit1 * gain_attn).astype(BF16)
    queries = nn(normed, w_query_ref[...]).astype(BF16)
    key_rows = nn(normed, w_key_ref[...]).astype(BF16)
    value_rows = nn(normed, w_value_ref[...]).astype(BF16)

    lane_head = lax.broadcasted_iota(jnp.int32, (length, width), 1) // head_width
    causal = lax.broadcasted_iota(jnp.int32, (length, length), 0) >= lax.broadcasted_iota(
        jnp.int32, (length, length), 1
    )
    scale = 1.0 / head_width**0.5

    def of_head(rows, h):
        return jnp.where(lane_head == h, rows, jnp.zeros_like(rows))

    attended = jnp.zeros((length, width), F32)
    for h in range(HEADS):
        scores = nt(of_head(queries, h), key_rows) * scale
        scores = jnp.where(causal, scores, -1e30)
        expo = jnp.exp(scores - jnp.max(scores, axis=1, keepdims=True))
        prob = expo / jnp.sum(expo, axis=1, keepdims=True)
        prob_ref[h] = prob
        attended = attended + nn(prob.astype(BF16), of_head(value_rows, h))
    attended = attended.astype(BF16)
    hidden1 = hidden0 + nn(attended, w_proj_ref[...])

    line = lax.broadcasted_iota(jnp.int32, (2 * length, length), 0)
    place = relay_ref[...] == line // (2 * share) * share + line % share
    moved = nn(place.astype(BF16), hidden1.astype(BF16))
    line = lax.broadcasted_iota(jnp.int32, (2 * length, 128), 0)
    left = line // share % 2 == 0
    relayed_ref[...] = jnp.where(left, moved[:, :128], moved[:, 128:]).astype(BF16)

    gain_out = gain_out_ref[...]
    inv2 = lax.rsqrt(jnp.mean(hidden1 * hidden1, axis=1, keepdims=True) + 1e-06)
    unit2 = hidden1 * inv2
    normed_out = (unit2 * gain_out).astype(BF16)
    logits = nn(normed_out, w_logit_ref[...])
    symbol = lax.broadcasted_iota(jnp.int32, logits.shape, 1)
    target = symbol == ids[:, kc : kc + 1]
    logit_max = jnp.max(logits, axis=1, keepdims=True)
    expo = jnp.exp(logits - logit_max)
    total = jnp.sum(expo, axis=1, keepdims=True)
    picked = jnp.sum(jnp.where(target, logits, 0.0), axis=1, keepdims=True)
    losses = logit_max + jnp.log(total) - picked
    lane = lax.broadcasted_iota(jnp.int32, (length, 128), 1)
    own_lane = lax.broadcasted_iota(jnp.int32, (length, 128), 0) % 128 == lane
    loss = jnp.sum(jnp.where(own_lane, losses, 0.0), axis=0, keepdims=True) * (1.0 / node_total)

    g_logits = ((expo / total - target.astype(F32)) * (1.0 / node_total)).astype(BF16)
    g_w_logit = tn(normed_out, g_logits).astype(BF16)
    g_normed_out = nt(g_logits, w_logit_ref[...]).astype(BF16).astype(F32)
    g_gain_out = jnp.sum(g_normed_out * unit2, axis=0, keepdims=True)
    g_unit = g_normed_out * gain_out
    g_hidden1 = inv2 * (g_unit - unit2 * jnp.mean(g_unit * unit2, axis=1, keepdims=True))
    g_rows = g_hidden1.astype(BF16)
    g_w_proj = tn(attended, g_rows).astype(BF16)
    g_attended = nt(g_rows, w_proj_ref[...]).astype(BF16)

    g_queries = jnp.zeros((length, width), F32)
    g_keys = jnp.zeros((length, width), F32)
    g_values = jnp.zeros((length, width), F32)
    for h in range(HEADS):
        prob = prob_ref[h]
        g_att_h = of_head(g_attended, h)
        g_prob = nt(g_att_h, value_rows).astype(BF16).astype(F32)
        g_values = g_values + tn(prob.astype(BF16), g_att_h)
        weighed = jnp.sum(g_prob * prob, axis=1, keepdims=True)
        g_scores = (prob * (g_prob - weighed) * scale).astype(BF16)
        g_queries = g_queries + nn(g_scores, of_head(key_rows, h))
        g_keys = g_keys + tn(g_scores, of_head(queries, h))
    g_queries = g_queries.astype(BF16)
    g_keys = g_keys.astype(BF16)
    g_values = g_values.astype(BF16)
    g_w_query = tn(normed, g_queries).astype(BF16)
    g_w_key = tn(normed, g_keys).astype(BF16)
    g_w_value = tn(normed, g_values).astype(BF16)
    g_normed = (
        nt(g_queries, w_query_ref[...])
        + nt(g_keys, w_key_ref[...])
        + nt(g_values, w_value_ref[...])
    )
    g_gain_attn = jnp.sum(g_normed * unit1, axis=0, keepdims=True)
    g_unit = g_normed * gain_attn
    g_hidden0 = g_hidden1 + inv1 * (
        g_unit - unit1 * jnp.mean(g_unit * unit1, axis=1, keepdims=True)
    )
    g_rows = g_hidden0.astype(BF16)
    for k in range(kc):
        g_w_ctx = tn(contexts[k], g_rows).astype(BF16)
        slab_ref[0, k * width : (k + 1) * width, :] = g_w_ctx[:, :128]
        slab_ref[0, (kc + k) * width : (kc + k + 1) * width, :] = g_w_ctx[:, 128:]
    first = 2 * kc * width
    slab_ref[0, first : first + width, :] = g_w_logit[:, :128]
    slab_ref[1, 0:width, :] = g_w_logit[:, 128:]
    row = width
    for grad in (g_w_query, g_w_key, g_w_value, g_w_proj):
        slab_ref[1, row : row + width, :] = grad[:, :128]
        slab_ref[1, row + width : row + 2 * width, :] = grad[:, 128:]
        row += 2 * width
    extra_ref[...] = jnp.zeros_like(extra_ref)
    extra_ref[0:1, :] = g_gain_attn[:, :128]
    extra_ref[1:2, :] = g_gain_attn[:, 128:]
    extra_ref[2:3, :] = g_gain_out[:, :128]
    extra_ref[3:4, :] = g_gain_out[:, 128:]
    extra_ref[4:5, :] = loss
    used = first + width
    slab_ref[0, used : used + 16, :] = extra_ref[...].astype(BF16)
    half = slab_ref.shape[1]
    slab_ref[0, used + 16 :, :] = jnp.zeros((half - used - 16, 128), BF16)
    slab_ref[1, used:, :] = jnp.zeros((half - used, 128), BF16)


def unpack_kernel(
    share,
    core_ref,
    own_ref,
    own_rows_ref,
    other_ref,
    relayed_ref,
    ctx_ref,
    query_ref,
    key_ref,
    value_ref,
    proj_ref,
    logit_ref,
    attn_ref,
    out_ref,
    loss_ref,
):
    core = core_ref[0]
    rows = ctx_ref.shape[0]
    width = logit_ref.shape[0]
    half = own_ref.shape[0]

    def lines(h, start, count):
        mine = own_ref[start : start + count, :].astype(F32)
        theirs = other_ref[start : start + count, :].astype(F32)
        return jnp.where(core == h, mine, theirs)

    for row in range(0, rows, width):
        ctx_ref[row : row + width, :128] = lines(0, row, width)
        ctx_ref[row : row + width, 128:] = lines(0, rows + row, width)
    logit_ref[:, :128] = lines(0, 2 * rows, width)
    logit_ref[:, 128:] = lines(1, 0, width)
    row = width
    for ref in (query_ref, key_ref, value_ref, proj_ref):
        ref[:, :128] = lines(1, row, width)
        ref[:, 128:] = lines(1, row + width, width)
        row += 2 * width
    extra = lines(0, 2 * rows + width, 16)
    attn_ref[:, :128] = extra[0:1]
    attn_ref[:, 128:] = extra[1:2]
    out_ref[:, :128] = extra[2:3]
    out_ref[:, 128:] = extra[3:4]
    loss_ref[...] = jnp.sum(extra[4:5], axis=1, keepdims=True)

    length = relayed_ref.shape[0]
    row = lax.broadcasted_iota(jnp.int32, (length, 2 * length), 0)
    line = lax.broadcasted_iota(jnp.int32, (length, 2 * length), 1)
    mine = row // share % 2 == core
    own_rows = own_rows_ref[...]
    other_rows = other_ref[half:, :]
    for h in range(2):
        found = line == (row // (2 * share) * 4 + 2 * core + h) * share + row % share
        here = (found & mine).astype(BF16)
        there = (found & ~mine).astype(BF16)
        relayed_ref[:, h * 128 : (h + 1) * 128] = (
            nn(here, own_rows) + nn(there, other_rows)
        ).astype(BF16)


def body(
    node_feats,
    ctx_table,
    fetch_rows,
    ctx_slot,
    labels,
    relay_slot,
    w_ctx,
    w_query,
    w_key,
    w_value,
    w_proj,
    w_logit,
    gain_attn,
    gain_out,
):
    features = node_feats[0]
    length, width = features.shape
    chips, ranges = lax.axis_size("chip"), lax.axis_size(RANGE)
    table = ctx_table[0]
    requests = fetch_rows[0, 0]
    cap = requests.shape[1]
    tiles = lax.axis_size("dp")
    share = length // ranges
    core = lax.axis_index("core").astype(jnp.int32).reshape(1)
    half = (w_ctx.shape[0] * width + 5 * width * width) // 256 + 16
    half = -(-half // (2 * tiles * chips)) * (2 * tiles * chips)
    quarter = half // tiles
    pairs = quarter // (2 * chips)
    moved_pairs = length // chips
    swap = [(0, 1), (1, 0)]
    vmem = pl.BlockSpec(memory_space=pltpu.VMEM)
    params = pltpu.CompilerParams(vmem_limit_bytes=32 * 1024 * 1024)

    smem = pl.BlockSpec(memory_space=pltpu.SMEM)

    def exchange(lines, axis):
        return lax.all_to_all(lines, axis, split_axis=0, concat_axis=0, tiled=True)

    asks, held = pl.pallas_call(
        ask_kernel,
        out_shape=(
            jax.ShapeDtypeStruct((ranges, 128), jnp.int32),
            jax.ShapeDtypeStruct(table.shape, BF16),
        ),
        in_specs=[vmem] * 2,
        out_specs=(vmem,) * 2,
        compiler_params=params,
        name="ask_rows",
    )(jnp.transpose(requests), table)
    asked = exchange(asks.reshape(chips, 2, 128), "chip")
    other_table = lax.ppermute(held, "core", swap)
    picked = pl.pallas_call(
        pick_kernel,
        out_shape=jax.ShapeDtypeStruct((ranges * cap, width), BF16),
        in_specs=[smem] + [vmem] * 3,
        out_specs=vmem,
        compiler_params=params,
        name="pick_rows",
    )(core, asked.reshape(ranges, 128), held, other_table)
    buffer = exchange(picked.reshape(chips, 2 * cap, width), "chip").reshape(ranges * cap, width)

    slab, moved = pl.pallas_call(
        functools.partial(step_kernel, float(length * ranges * tiles), share),
        out_shape=(
            jax.ShapeDtypeStruct((2, half, 128), BF16),
            jax.ShapeDtypeStruct((2 * length, 128), BF16),
        ),
        in_specs=[vmem] * 13,
        out_specs=(vmem, vmem),
        scratch_shapes=[
            pltpu.VMEM((8, length), jnp.int32),
            pltpu.VMEM((16, 128), F32),
            pltpu.VMEM((HEADS, length, length), F32),
        ],
        compiler_params=params,
        name="window_step",
    )(
        features,
        buffer,
        jnp.transpose(ctx_slot[0]),
        labels,
        relay_slot,
        w_ctx,
        w_query,
        w_key,
        w_value,
        w_proj,
        w_logit,
        gain_attn.reshape(1, width),
        gain_out.reshape(1, width),
    )

    def total(parts):
        return lax.optimization_barrier(jnp.sum(parts.astype(F32), axis=0)).astype(BF16)

    part = total(exchange(slab.reshape(2 * tiles, quarter, 128), ("core", "dp")))
    piece = total(exchange(part.reshape(chips, pairs, 2, 128), "chip"))

    repeated = jnp.broadcast_to(piece[None], (chips, pairs, 2, 128))
    moved = moved.reshape(chips, moved_pairs, 2, 128)
    parts = exchange(jnp.concatenate([repeated, moved], axis=1), "chip")
    own_rows = parts[:, pairs:].reshape(2 * length, 128)
    part = jnp.broadcast_to(parts[:, :pairs].reshape(1, quarter, 128), (tiles, quarter, 128))
    own = exchange(part, "dp").reshape(half, 128)
    other = lax.ppermute(jnp.concatenate([own, own_rows], axis=0), "core", swap)

    square = jax.ShapeDtypeStruct((width, width), F32)
    line = jax.ShapeDtypeStruct((1, width), F32)
    outs = pl.pallas_call(
        functools.partial(unpack_kernel, share),
        out_shape=(
            jax.ShapeDtypeStruct((length, width), BF16),
            jax.ShapeDtypeStruct(w_ctx.shape, F32),
        )
        + (square,) * 5
        + (line, line, jax.ShapeDtypeStruct((1, 1), F32)),
        in_specs=[smem] + [vmem] * 3,
        out_specs=(vmem,) * 10,
        compiler_params=params,
        name="unpack",
    )(core, own, own_rows, other)
    return (
        outs[0][None],
        outs[9].reshape(()),
        outs[1],
        outs[2],
        outs[3],
        outs[4],
        outs[5],
        outs[6],
        outs[7].reshape(width),
        outs[8].reshape(width),
    )


def solution(mesh):
    ranges, tiles = mesh.devices.shape
    split = jax.sharding.Mesh(
        mesh.devices.reshape(ranges // 2, 2, tiles), ("chip", "core", "dp")
    )
    placed = (
        P("dp", RANGE, None),
        P("dp", RANGE, None),
        P("dp", RANGE, None, None),
        P("dp", RANGE, None),
        P("dp", RANGE),
        P("dp", RANGE),
        P(),
        P(),
        P(),
        P(),
        P(),
        P(),
        P(),
        P(),
    )
    return jax.shard_map(
        body,
        mesh=split,
        in_specs=placed,
        out_specs=(P("dp", RANGE, None), P(), P(), P(), P(), P(), P(), P(), P(), P()),
        check_vma=False,
    )
```

```python
import functools

import jax
import jax.numpy as jnp
from jax import lax
from jax.experimental import pallas as pl
from jax.experimental.pallas import tpu as pltpu
from jax.sharding import PartitionSpec as P

HEADS = 4
RANGE = ("chip", "core")
F32 = jnp.float32
BF16 = jnp.bfloat16


def nn(a, b):
    return lax.dot_general(a, b, (((1,), (0,)), ((), ())), preferred_element_type=F32)


def nt(a, b):
    return lax.dot_general(a, b, (((1,), (1,)), ((), ())), preferred_element_type=F32)


def tn(a, b):
    return lax.dot_general(a, b, (((0,), (0,)), ((), ())), preferred_element_type=F32)


def ask_kernel(asks_ref, table_ref, out_ref, held_ref):
    cap, owners = asks_ref.shape
    lines = jnp.concatenate([asks_ref[...], jnp.zeros((128 - cap, owners), jnp.int32)], axis=0)
    out_ref[...] = jnp.transpose(lines)
    held_ref[...] = table_ref[...]


def pick_kernel(core_ref, idx_ref, own_ref, other_ref, out_ref):
    asks, lanes = idx_ref.shape
    rows = out_ref.shape[0]
    cap = rows // asks
    line = lax.broadcasted_iota(jnp.int32, (rows, asks), 0)
    spread = (line // cap == lax.broadcasted_iota(jnp.int32, (rows, asks), 1)).astype(BF16)
    ids = nn(spread, idx_ref[...].astype(F32).astype(BF16))
    own = lax.broadcasted_iota(jnp.int32, (rows, lanes), 0) % cap == lax.broadcasted_iota(
        jnp.int32, (rows, lanes), 1
    )
    ids = jnp.sum(jnp.where(own, ids, 0.0), axis=1, keepdims=True).astype(jnp.int32)
    hot = ids == lax.broadcasted_iota(jnp.int32, (rows, own_ref.shape[0]), 1)
    mine = lax.broadcasted_iota(jnp.int32, hot.shape, 0) // cap % 2 == core_ref[0]
    out_ref[...] = (
        nn((hot & mine).astype(BF16), own_ref[...])
        + nn((hot & ~mine).astype(BF16), other_ref[...])
    ).astype(BF16)


def step_kernel(
    node_total,
    share,
    core_ref,
    feats_ref,
    buf_ref,
    slot_ref,
    label_ref,
    relay_ref,
    w_ctx_ref,
    w_query_ref,
    w_key_ref,
    w_value_ref,
    w_proj_ref,
    w_logit_ref,
    gain_attn_ref,
    gain_out_ref,
    slab_ref,
    relayed_ref,
    ids_ref,
    extra_ref,
    prob_ref,
):
    length, width = feats_ref.shape
    slots = buf_ref.shape[0]
    kc = slot_ref.shape[0]
    head_width = width // HEADS

    ids_ref[0:kc, :] = slot_ref[...]
    ids_ref[kc : kc + 1, :] = label_ref[...]
    ids_ref[kc + 1 :, :] = jnp.zeros((8 - kc - 1, length), jnp.int32)
    ids = jnp.transpose(ids_ref[...])

    buf = buf_ref[...]
    slot_lane = lax.broadcasted_iota(jnp.int32, (length, slots), 1)
    contexts = []
    hidden0 = feats_ref[...].astype(F32)
    for k in range(kc):
        hot = (ids[:, k : k + 1] == slot_lane).astype(BF16)
        part = nn(hot, buf).astype(BF16)
        contexts.append(part)
        hidden0 = hidden0 + nn(part, w_ctx_ref[k * width : (k + 1) * width, :])

    gain_attn = gain_attn_ref[...]
    inv1 = lax.rsqrt(jnp.mean(hidden0 * hidden0, axis=1, keepdims=True) + 1e-06)
    unit1 = hidden0 * inv1
    normed = (unit1 * gain_attn).astype(BF16)
    queries = nn(normed, w_query_ref[...]).astype(BF16)
    key_rows = nn(normed, w_key_ref[...]).astype(BF16)
    value_rows = nn(normed, w_value_ref[...]).astype(BF16)

    lane_head = lax.broadcasted_iota(jnp.int32, (length, width), 1) // head_width
    causal = lax.broadcasted_iota(jnp.int32, (length, length), 0) >= lax.broadcasted_iota(
        jnp.int32, (length, length), 1
    )
    scale = 1.0 / head_width**0.5

    def of_head(rows, h):
        return jnp.where(lane_head == h, rows, jnp.zeros_like(rows))

    attended = jnp.zeros((length, width), F32)
    for h in range(HEADS):
        scores = nt(of_head(queries, h), key_rows) * scale
        scores = jnp.where(causal, scores, -1e30)
        expo = jnp.exp(scores - jnp.max(scores, axis=1, keepdims=True))
        prob = expo / jnp.sum(expo, axis=1, keepdims=True)
        prob_ref[h] = prob
        attended = attended + nn(prob.astype(BF16), of_head(value_rows, h))
    attended = attended.astype(BF16)
    hidden1 = hidden0 + nn(attended, w_proj_ref[...])

    line = lax.broadcasted_iota(jnp.int32, (2 * length, length), 0)
    place = relay_ref[...] == line // (2 * share) * share + line % share
    moved = nn(place.astype(BF16), hidden1.astype(BF16))
    line = lax.broadcasted_iota(jnp.int32, (2 * length, 128), 0)
    left = line // share % 2 == 0
    relayed_ref[...] = jnp.where(left, moved[:, :128], moved[:, 128:]).astype(BF16)

    gain_out = gain_out_ref[...]
    inv2 = lax.rsqrt(jnp.mean(hidden1 * hidden1, axis=1, keepdims=True) + 1e-06)
    unit2 = hidden1 * inv2
    normed_out = (unit2 * gain_out).astype(BF16)
    logits = nn(normed_out, w_logit_ref[...])
    symbol = lax.broadcasted_iota(jnp.int32, logits.shape, 1)
    target = symbol == ids[:, kc : kc + 1]
    logit_max = jnp.max(logits, axis=1, keepdims=True)
    expo = jnp.exp(logits - logit_max)
    total = jnp.sum(expo, axis=1, keepdims=True)
    picked = jnp.sum(jnp.where(target, logits, 0.0), axis=1, keepdims=True)
    losses = logit_max + jnp.log(total) - picked
    lane = lax.broadcasted_iota(jnp.int32, (length, 128), 1)
    own_lane = lax.broadcasted_iota(jnp.int32, (length, 128), 0) % 128 == lane
    loss = jnp.sum(jnp.where(own_lane, losses, 0.0), axis=0, keepdims=True) * (1.0 / node_total)

    g_logits = ((expo / total - target.astype(F32)) * (1.0 / node_total)).astype(BF16)
    g_w_logit = tn(normed_out, g_logits).astype(BF16)
    g_normed_out = nt(g_logits, w_logit_ref[...]).astype(BF16).astype(F32)
    g_gain_out = jnp.sum(g_normed_out * unit2, axis=0, keepdims=True)
    g_unit = g_normed_out * gain_out
    g_hidden1 = inv2 * (g_unit - unit2 * jnp.mean(g_unit * unit2, axis=1, keepdims=True))
    g_rows = g_hidden1.astype(BF16)
    g_w_proj = tn(attended, g_rows).astype(BF16)
    g_attended = nt(g_rows, w_proj_ref[...]).astype(BF16)

    g_queries = jnp.zeros((length, width), F32)
    g_keys = jnp.zeros((length, width), F32)
    g_values = jnp.zeros((length, width), F32)
    for h in range(HEADS):
        prob = prob_ref[h]
        g_att_h = of_head(g_attended, h)
        g_prob = nt(g_att_h, value_rows).astype(BF16).astype(F32)
        g_values = g_values + tn(prob.astype(BF16), g_att_h)
        weighed = jnp.sum(g_prob * prob, axis=1, keepdims=True)
        g_scores = (prob * (g_prob - weighed) * scale).astype(BF16)
        g_queries = g_queries + nn(g_scores, of_head(key_rows, h))
        g_keys = g_keys + tn(g_scores, of_head(queries, h))
    g_queries = g_queries.astype(BF16)
    g_keys = g_keys.astype(BF16)
    g_values = g_values.astype(BF16)
    g_w_query = tn(normed, g_queries).astype(BF16)
    g_w_key = tn(normed, g_keys).astype(BF16)
    g_w_value = tn(normed, g_values).astype(BF16)
    g_normed = (
        nt(g_queries, w_query_ref[...])
        + nt(g_keys, w_key_ref[...])
        + nt(g_values, w_value_ref[...])
    )
    g_gain_attn = jnp.sum(g_normed * unit1, axis=0, keepdims=True)
    g_unit = g_normed * gain_attn
    g_hidden0 = g_hidden1 + inv1 * (
        g_unit - unit1 * jnp.mean(g_unit * unit1, axis=1, keepdims=True)
    )
    g_rows = g_hidden0.astype(BF16)
    half = slab_ref.shape[1]
    core = core_ref[0]

    def put(h, row, lines):
        slab_ref[(core + h) % 2, row : row + lines.shape[0], :] = lines

    for k in range(kc):
        g_w_ctx = tn(contexts[k], g_rows).astype(BF16)
        put(0, k * width, g_w_ctx[:, :128])
        put(0, (kc + k) * width, g_w_ctx[:, 128:])
    first = 2 * kc * width
    put(0, first, g_w_logit[:, :128])
    put(1, 0, g_w_logit[:, 128:])
    row = width
    for grad in (g_w_query, g_w_key, g_w_value, g_w_proj):
        put(1, row, grad[:, :128])
        put(1, row + width, grad[:, 128:])
        row += 2 * width
    extra_ref[...] = jnp.zeros_like(extra_ref)
    extra_ref[0:1, :] = g_gain_attn[:, :128]
    extra_ref[1:2, :] = g_gain_attn[:, 128:]
    extra_ref[2:3, :] = g_gain_out[:, :128]
    extra_ref[3:4, :] = g_gain_out[:, 128:]
    extra_ref[4:5, :] = loss
    used = first + width
    put(0, used, extra_ref[...].astype(BF16))
    put(0, used + 16, jnp.zeros((half - used - 16, 128), BF16))
    put(1, used, jnp.zeros((half - used, 128), BF16))


def unpack_kernel(
    share,
    core_ref,
    own_ref,
    own_rows_ref,
    other_ref,
    relayed_ref,
    ctx_ref,
    query_ref,
    key_ref,
    value_ref,
    proj_ref,
    logit_ref,
    attn_ref,
    out_ref,
    loss_ref,
):
    core = core_ref[0]
    rows = ctx_ref.shape[0]
    width = logit_ref.shape[0]
    half = own_ref.shape[0]

    def lines(h, start, count):
        mine = own_ref[start : start + count, :].astype(F32)
        theirs = other_ref[start : start + count, :].astype(F32)
        return jnp.where(core == h, mine, theirs)

    for row in range(0, rows, width):
        ctx_ref[row : row + width, :128] = lines(0, row, width)
        ctx_ref[row : row + width, 128:] = lines(0, rows + row, width)
    logit_ref[:, :128] = lines(0, 2 * rows, width)
    logit_ref[:, 128:] = lines(1, 0, width)
    row = width
    for ref in (query_ref, key_ref, value_ref, proj_ref):
        ref[:, :128] = lines(1, row, width)
        ref[:, 128:] = lines(1, row + width, width)
        row += 2 * width
    extra = lines(0, 2 * rows + width, 16)
    attn_ref[:, :128] = extra[0:1]
    attn_ref[:, 128:] = extra[1:2]
    out_ref[:, :128] = extra[2:3]
    out_ref[:, 128:] = extra[3:4]
    loss_ref[...] = jnp.sum(extra[4:5], axis=1, keepdims=True)

    length = relayed_ref.shape[0]
    row = lax.broadcasted_iota(jnp.int32, (length, 2 * length), 0)
    line = lax.broadcasted_iota(jnp.int32, (length, 2 * length), 1)
    mine = row // share % 2 == core
    own_rows = own_rows_ref[...]
    other_rows = other_ref[half:, :]
    for h in range(2):
        found = line == (row // (2 * share) * 4 + 2 * core + h) * share + row % share
        here = (found & mine).astype(BF16)
        there = (found & ~mine).astype(BF16)
        relayed_ref[:, h * 128 : (h + 1) * 128] = (
            nn(here, own_rows) + nn(there, other_rows)
        ).astype(BF16)


def body(
    node_feats,
    ctx_table,
    fetch_rows,
    ctx_slot,
    labels,
    relay_slot,
    w_ctx,
    w_query,
    w_key,
    w_value,
    w_proj,
    w_logit,
    gain_attn,
    gain_out,
):
    features = node_feats[0]
    length, width = features.shape
    chips, ranges = lax.axis_size("chip"), lax.axis_size(RANGE)
    table = ctx_table[0]
    requests = fetch_rows[0, 0]
    cap = requests.shape[1]
    tiles = lax.axis_size("dp")
    share = length // ranges
    core = lax.axis_index("core").astype(jnp.int32).reshape(1)
    half = (w_ctx.shape[0] * width + 5 * width * width) // 256 + 16
    half = -(-half // (2 * tiles * chips)) * (2 * tiles * chips)
    quarter = half // tiles
    pairs = quarter // (2 * chips)
    moved_pairs = length // chips
    swap = [(0, 1), (1, 0)]
    vmem = pl.BlockSpec(memory_space=pltpu.VMEM)
    params = pltpu.CompilerParams(vmem_limit_bytes=32 * 1024 * 1024)

    smem = pl.BlockSpec(memory_space=pltpu.SMEM)

    def exchange(lines, axis):
        return lax.all_to_all(lines, axis, split_axis=0, concat_axis=0, tiled=True)

    asks, held = pl.pallas_call(
        ask_kernel,
        out_shape=(
            jax.ShapeDtypeStruct((ranges, 128), jnp.int32),
            jax.ShapeDtypeStruct(table.shape, BF16),
        ),
        in_specs=[vmem] * 2,
        out_specs=(vmem,) * 2,
        compiler_params=params,
        name="ask_rows",
    )(jnp.transpose(requests), table)
    asked = exchange(asks.reshape(chips, 2, 128), "chip")
    other_table = lax.ppermute(held, "core", swap)
    picked = pl.pallas_call(
        pick_kernel,
        out_shape=jax.ShapeDtypeStruct((ranges * cap, width), BF16),
        in_specs=[smem] + [vmem] * 3,
        out_specs=vmem,
        compiler_params=params,
        name="pick_rows",
    )(core, asked.reshape(ranges, 128), held, other_table)
    buffer = exchange(picked.reshape(chips, 2 * cap, width), "chip").reshape(ranges * cap, width)

    slab, moved = pl.pallas_call(
        functools.partial(step_kernel, float(length * ranges * tiles), share),
        out_shape=(
            jax.ShapeDtypeStruct((2, half, 128), BF16),
            jax.ShapeDtypeStruct((2 * length, 128), BF16),
        ),
        in_specs=[smem] + [vmem] * 13,
        out_specs=(vmem, vmem),
        scratch_shapes=[
            pltpu.VMEM((8, length), jnp.int32),
            pltpu.VMEM((16, 128), F32),
            pltpu.VMEM((HEADS, length, length), F32),
        ],
        compiler_params=params,
        name="window_step",
    )(
        core,
        features,
        buffer,
        jnp.transpose(ctx_slot[0]),
        labels,
        relay_slot,
        w_ctx,
        w_query,
        w_key,
        w_value,
        w_proj,
        w_logit,
        gain_attn.reshape(1, width),
        gain_out.reshape(1, width),
    )

    def total(parts):
        return lax.optimization_barrier(jnp.sum(parts.astype(F32), axis=0)).astype(BF16)

    other = lax.ppermute(slab[1], "core", swap)
    pair = (slab[0].astype(F32) + other.astype(F32)).astype(BF16)
    piece = total(exchange(pair.reshape(chips * tiles, pairs, 2, 128), ("chip", "dp")))

    repeated = jnp.broadcast_to(piece[None], (chips, pairs, 2, 128))
    moved = moved.reshape(chips, moved_pairs, 2, 128)
    parts = exchange(jnp.concatenate([repeated, moved], axis=1), "chip")
    part, own_rows = lax.optimization_barrier((parts[:, :pairs], parts[:, pairs:]))
    own = exchange(jnp.broadcast_to(part[None], (tiles, *part.shape)), "dp")
    own = own.swapaxes(0, 1).reshape(half, 128)
    own_rows = own_rows.reshape(2 * length, 128)
    other = lax.ppermute(jnp.concatenate([own, own_rows], axis=0), "core", swap)

    square = jax.ShapeDtypeStruct((width, width), F32)
    line = jax.ShapeDtypeStruct((1, width), F32)
    outs = pl.pallas_call(
        functools.partial(unpack_kernel, share),
        out_shape=(
            jax.ShapeDtypeStruct((length, width), BF16),
            jax.ShapeDtypeStruct(w_ctx.shape, F32),
        )
        + (square,) * 5
        + (line, line, jax.ShapeDtypeStruct((1, 1), F32)),
        in_specs=[smem] + [vmem] * 3,
        out_specs=(vmem,) * 10,
        compiler_params=params,
        name="unpack",
    )(core, own, own_rows, other)
    return (
        outs[0][None],
        outs[9].reshape(()),
        outs[1],
        outs[2],
        outs[3],
        outs[4],
        outs[5],
        outs[6],
        outs[7].reshape(width),
        outs[8].reshape(width),
    )


def solution(mesh):
    ranges, tiles = mesh.devices.shape
    split = jax.sharding.Mesh(
        mesh.devices.reshape(ranges // 2, 2, tiles), ("chip", "core", "dp")
    )
    placed = (
        P("dp", RANGE, None),
        P("dp", RANGE, None),
        P("dp", RANGE, None, None),
        P("dp", RANGE, None),
        P("dp", RANGE),
        P("dp", RANGE),
        P(),
        P(),
        P(),
        P(),
        P(),
        P(),
        P(),
        P(),
    )
    return jax.shard_map(
        body,
        mesh=split,
        in_specs=placed,
        out_specs=(P("dp", RANGE, None), P(), P(), P(), P(), P(), P(), P(), P(), P()),
        check_vma=False,
    )
```

```python
import functools

import jax
import jax.numpy as jnp
from jax import lax
from jax.experimental import pallas as pl
from jax.experimental.pallas import tpu as pltpu
from jax.sharding import PartitionSpec as P

HEADS = 4
RANGE = ("chip", "core")
F32 = jnp.float32
BF16 = jnp.bfloat16


def nn(a, b):
    return lax.dot_general(a, b, (((1,), (0,)), ((), ())), preferred_element_type=F32)


def nt(a, b):
    return lax.dot_general(a, b, (((1,), (1,)), ((), ())), preferred_element_type=F32)


def tn(a, b):
    return lax.dot_general(a, b, (((0,), (0,)), ((), ())), preferred_element_type=F32)


def ask_kernel(asks_ref, table_ref, out_ref, held_ref):
    cap, owners = asks_ref.shape
    lines = jnp.concatenate([asks_ref[...], jnp.zeros((128 - cap, owners), jnp.int32)], axis=0)
    out_ref[...] = jnp.transpose(lines)
    held_ref[...] = table_ref[...]


def pick_kernel(core_ref, idx_ref, own_ref, other_ref, out_ref):
    asks, lanes = idx_ref.shape
    rows = out_ref.shape[0]
    cap = rows // asks
    line = lax.broadcasted_iota(jnp.int32, (rows, asks), 0)
    spread = (line // cap == lax.broadcasted_iota(jnp.int32, (rows, asks), 1)).astype(BF16)
    ids = nn(spread, idx_ref[...].astype(F32).astype(BF16))
    own = lax.broadcasted_iota(jnp.int32, (rows, lanes), 0) % cap == lax.broadcasted_iota(
        jnp.int32, (rows, lanes), 1
    )
    ids = jnp.sum(jnp.where(own, ids, 0.0), axis=1, keepdims=True).astype(jnp.int32)
    hot = ids == lax.broadcasted_iota(jnp.int32, (rows, own_ref.shape[0]), 1)
    mine = lax.broadcasted_iota(jnp.int32, hot.shape, 0) // cap % 2 == core_ref[0]
    out_ref[...] = (
        nn((hot & mine).astype(BF16), own_ref[...])
        + nn((hot & ~mine).astype(BF16), other_ref[...])
    ).astype(BF16)


def step_kernel(
    node_total,
    share,
    core_ref,
    feats_ref,
    buf_ref,
    slot_ref,
    label_ref,
    relay_ref,
    w_ctx_ref,
    w_query_ref,
    w_key_ref,
    w_value_ref,
    w_proj_ref,
    w_logit_ref,
    gain_attn_ref,
    gain_out_ref,
    slab_ref,
    relayed_ref,
    ids_ref,
    extra_ref,
    prob_ref,
):
    length, width = feats_ref.shape
    slots = buf_ref.shape[0]
    kc = slot_ref.shape[0]
    head_width = width // HEADS

    ids_ref[0:kc, :] = slot_ref[...]
    ids_ref[kc : kc + 1, :] = label_ref[...]
    ids_ref[kc + 1 :, :] = jnp.zeros((8 - kc - 1, length), jnp.int32)
    ids = jnp.transpose(ids_ref[...])

    buf = buf_ref[...]
    slot_lane = lax.broadcasted_iota(jnp.int32, (length, slots), 1)
    contexts = []
    hidden0 = feats_ref[...].astype(F32)
    for k in range(kc):
        hot = (ids[:, k : k + 1] == slot_lane).astype(BF16)
        part = nn(hot, buf).astype(BF16)
        contexts.append(part)
        hidden0 = hidden0 + nn(part, w_ctx_ref[k * width : (k + 1) * width, :])

    gain_attn = gain_attn_ref[...]
    inv1 = lax.rsqrt(jnp.mean(hidden0 * hidden0, axis=1, keepdims=True) + 1e-06)
    unit1 = hidden0 * inv1
    normed = (unit1 * gain_attn).astype(BF16)
    queries = nn(normed, w_query_ref[...]).astype(BF16)
    key_rows = nn(normed, w_key_ref[...]).astype(BF16)
    value_rows = nn(normed, w_value_ref[...]).astype(BF16)

    lane_head = lax.broadcasted_iota(jnp.int32, (length, width), 1) // head_width
    causal = lax.broadcasted_iota(jnp.int32, (length, length), 0) >= lax.broadcasted_iota(
        jnp.int32, (length, length), 1
    )
    scale = 1.0 / head_width**0.5

    def of_head(rows, h):
        return jnp.where(lane_head == h, rows, jnp.zeros_like(rows))

    attended = jnp.zeros((length, width), F32)
    for h in range(HEADS):
        scores = nt(of_head(queries, h), key_rows) * scale
        scores = jnp.where(causal, scores, -1e30)
        expo = jnp.exp(scores - jnp.max(scores, axis=1, keepdims=True))
        prob = expo / jnp.sum(expo, axis=1, keepdims=True)
        prob_ref[h] = prob
        attended = attended + nn(prob.astype(BF16), of_head(value_rows, h))
    attended = attended.astype(BF16)
    hidden1 = hidden0 + nn(attended, w_proj_ref[...])

    line = lax.broadcasted_iota(jnp.int32, (2 * length, length), 0)
    place = relay_ref[...] == line // (2 * share) * share + line % share
    moved = nn(place.astype(BF16), hidden1.astype(BF16))
    line = lax.broadcasted_iota(jnp.int32, (2 * length, 128), 0)
    left = line // share % 2 == 0
    relayed_ref[...] = jnp.where(left, moved[:, :128], moved[:, 128:]).astype(BF16)

    gain_out = gain_out_ref[...]
    inv2 = lax.rsqrt(jnp.mean(hidden1 * hidden1, axis=1, keepdims=True) + 1e-06)
    unit2 = hidden1 * inv2
    normed_out = (unit2 * gain_out).astype(BF16)
    logits = nn(normed_out, w_logit_ref[...])
    symbol = lax.broadcasted_iota(jnp.int32, logits.shape, 1)
    target = symbol == ids[:, kc : kc + 1]
    logit_max = jnp.max(logits, axis=1, keepdims=True)
    expo = jnp.exp(logits - logit_max)
    total = jnp.sum(expo, axis=1, keepdims=True)
    picked = jnp.sum(jnp.where(target, logits, 0.0), axis=1, keepdims=True)
    losses = logit_max + jnp.log(total) - picked
    lane = lax.broadcasted_iota(jnp.int32, (length, 128), 1)
    own_lane = lax.broadcasted_iota(jnp.int32, (length, 128), 0) % 128 == lane
    loss = jnp.sum(jnp.where(own_lane, losses, 0.0), axis=0, keepdims=True) * (1.0 / node_total)

    g_logits = ((expo / total - target.astype(F32)) * (1.0 / node_total)).astype(BF16)
    g_w_logit = tn(normed_out, g_logits).astype(BF16)
    g_normed_out = nt(g_logits, w_logit_ref[...]).astype(BF16).astype(F32)
    g_gain_out = jnp.sum(g_normed_out * unit2, axis=0, keepdims=True)
    g_unit = g_normed_out * gain_out
    g_hidden1 = inv2 * (g_unit - unit2 * jnp.mean(g_unit * unit2, axis=1, keepdims=True))
    g_rows = g_hidden1.astype(BF16)
    g_w_proj = tn(attended, g_rows).astype(BF16)
    g_attended = nt(g_rows, w_proj_ref[...]).astype(BF16)

    g_queries = jnp.zeros((length, width), F32)
    g_keys = jnp.zeros((length, width), F32)
    g_values = jnp.zeros((length, width), F32)
    for h in range(HEADS):
        prob = prob_ref[h]
        g_att_h = of_head(g_attended, h)
        g_prob = nt(g_att_h, value_rows).astype(BF16).astype(F32)
        g_values = g_values + tn(prob.astype(BF16), g_att_h)
        weighed = jnp.sum(g_prob * prob, axis=1, keepdims=True)
        g_scores = (prob * (g_prob - weighed) * scale).astype(BF16)
        g_queries = g_queries + nn(g_scores, of_head(key_rows, h))
        g_keys = g_keys + tn(g_scores, of_head(queries, h))
    g_queries = g_queries.astype(BF16)
    g_keys = g_keys.astype(BF16)
    g_values = g_values.astype(BF16)
    g_w_query = tn(normed, g_queries).astype(BF16)
    g_w_key = tn(normed, g_keys).astype(BF16)
    g_w_value = tn(normed, g_values).astype(BF16)
    g_normed = (
        nt(g_queries, w_query_ref[...])
        + nt(g_keys, w_key_ref[...])
        + nt(g_values, w_value_ref[...])
    )
    g_gain_attn = jnp.sum(g_normed * unit1, axis=0, keepdims=True)
    g_unit = g_normed * gain_attn
    g_hidden0 = g_hidden1 + inv1 * (
        g_unit - unit1 * jnp.mean(g_unit * unit1, axis=1, keepdims=True)
    )
    g_rows = g_hidden0.astype(BF16)
    half = slab_ref.shape[1]
    core = core_ref[0]

    def put(h, row, lines):
        slab_ref[(core + h) % 2, row : row + lines.shape[0], :] = lines

    for k in range(kc):
        g_w_ctx = tn(contexts[k], g_rows).astype(BF16)
        put(0, k * width, g_w_ctx[:, :128])
        put(0, (kc + k) * width, g_w_ctx[:, 128:])
    first = 2 * kc * width
    put(0, first, g_w_logit[:, :128])
    put(1, 0, g_w_logit[:, 128:])
    row = width
    for grad in (g_w_query, g_w_key, g_w_value, g_w_proj):
        put(1, row, grad[:, :128])
        put(1, row + width, grad[:, 128:])
        row += 2 * width
    extra_ref[...] = jnp.zeros_like(extra_ref)
    extra_ref[0:1, :] = g_gain_attn[:, :128]
    extra_ref[1:2, :] = g_gain_attn[:, 128:]
    extra_ref[2:3, :] = g_gain_out[:, :128]
    extra_ref[3:4, :] = g_gain_out[:, 128:]
    extra_ref[4:5, :] = loss
    used = first + width
    put(0, used, extra_ref[...].astype(BF16))
    put(0, used + 16, jnp.zeros((half - used - 16, 128), BF16))
    put(1, used, jnp.zeros((half - used, 128), BF16))


def unpack_kernel(
    share,
    core_ref,
    own_ref,
    own_rows_ref,
    other_ref,
    relayed_ref,
    ctx_ref,
    query_ref,
    key_ref,
    value_ref,
    proj_ref,
    logit_ref,
    attn_ref,
    out_ref,
    loss_ref,
):
    core = core_ref[0]
    rows = ctx_ref.shape[0]
    width = logit_ref.shape[0]
    half = own_ref.shape[0]

    def lines(h, start, count):
        mine = own_ref[start : start + count, :].astype(F32)
        theirs = other_ref[start : start + count, :].astype(F32)
        return jnp.where(core == h, mine, theirs)

    for row in range(0, rows, width):
        ctx_ref[row : row + width, :128] = lines(0, row, width)
        ctx_ref[row : row + width, 128:] = lines(0, rows + row, width)
    logit_ref[:, :128] = lines(0, 2 * rows, width)
    logit_ref[:, 128:] = lines(1, 0, width)
    row = width
    for ref in (query_ref, key_ref, value_ref, proj_ref):
        ref[:, :128] = lines(1, row, width)
        ref[:, 128:] = lines(1, row + width, width)
        row += 2 * width
    extra = lines(0, 2 * rows + width, 16)
    attn_ref[:, :128] = extra[0:1]
    attn_ref[:, 128:] = extra[1:2]
    out_ref[:, :128] = extra[2:3]
    out_ref[:, 128:] = extra[3:4]
    loss_ref[...] = jnp.sum(extra[4:5], axis=1, keepdims=True)

    length = relayed_ref.shape[0]
    row = lax.broadcasted_iota(jnp.int32, (length, 2 * length), 0)
    line = lax.broadcasted_iota(jnp.int32, (length, 2 * length), 1)
    mine = row // share % 2 == core
    own_rows = own_rows_ref[...]
    other_rows = other_ref[half:, :]
    for h in range(2):
        found = line == (row // (2 * share) * 4 + 2 * core + h) * share + row % share
        here = (found & mine).astype(BF16)
        there = (found & ~mine).astype(BF16)
        relayed_ref[:, h * 128 : (h + 1) * 128] = (
            nn(here, own_rows) + nn(there, other_rows)
        ).astype(BF16)


def body(
    node_feats,
    ctx_table,
    fetch_rows,
    ctx_slot,
    labels,
    relay_slot,
    w_ctx,
    w_query,
    w_key,
    w_value,
    w_proj,
    w_logit,
    gain_attn,
    gain_out,
):
    features = node_feats[0]
    length, width = features.shape
    chips, ranges = lax.axis_size("chip"), lax.axis_size(RANGE)
    table = ctx_table[0]
    requests = fetch_rows[0, 0]
    cap = requests.shape[1]
    tiles = lax.axis_size("dp")
    share = length // ranges
    core = lax.axis_index("core").astype(jnp.int32).reshape(1)
    half = (w_ctx.shape[0] * width + 5 * width * width) // 256 + 16
    half = -(-half // (2 * tiles * chips)) * (2 * tiles * chips)
    quarter = half // tiles
    pairs = quarter // (2 * chips)
    moved_pairs = length // chips
    swap = [(0, 1), (1, 0)]
    vmem = pl.BlockSpec(memory_space=pltpu.VMEM)
    params = pltpu.CompilerParams(vmem_limit_bytes=32 * 1024 * 1024)

    smem = pl.BlockSpec(memory_space=pltpu.SMEM)

    def exchange(lines, axis):
        return lax.all_to_all(lines, axis, split_axis=0, concat_axis=0, tiled=True)

    asks, held = pl.pallas_call(
        ask_kernel,
        out_shape=(
            jax.ShapeDtypeStruct((ranges, 128), jnp.int32),
            jax.ShapeDtypeStruct(table.shape, BF16),
        ),
        in_specs=[vmem] * 2,
        out_specs=(vmem,) * 2,
        compiler_params=params,
        name="ask_rows",
    )(jnp.transpose(requests), table)
    asked = exchange(asks.reshape(chips, 2, 128), "chip")
    other_table = lax.ppermute(held, "core", swap)
    picked = pl.pallas_call(
        pick_kernel,
        out_shape=jax.ShapeDtypeStruct((ranges * cap, width), BF16),
        in_specs=[smem] + [vmem] * 3,
        out_specs=vmem,
        compiler_params=params,
        name="pick_rows",
    )(core, asked.reshape(ranges, 128), held, other_table)
    buffer = exchange(picked.reshape(chips, 2 * cap, width), "chip").reshape(ranges * cap, width)

    slab, moved = pl.pallas_call(
        functools.partial(step_kernel, float(length * ranges * tiles), share),
        out_shape=(
            jax.ShapeDtypeStruct((2, half, 128), BF16),
            jax.ShapeDtypeStruct((2 * length, 128), BF16),
        ),
        in_specs=[smem] + [vmem] * 13,
        out_specs=(vmem, vmem),
        scratch_shapes=[
            pltpu.VMEM((8, length), jnp.int32),
            pltpu.VMEM((16, 128), F32),
            pltpu.VMEM((HEADS, length, length), F32),
        ],
        compiler_params=params,
        name="window_step",
    )(
        core,
        features,
        buffer,
        jnp.transpose(ctx_slot[0]),
        labels,
        relay_slot,
        w_ctx,
        w_query,
        w_key,
        w_value,
        w_proj,
        w_logit,
        gain_attn.reshape(1, width),
        gain_out.reshape(1, width),
    )

    def total(parts):
        return lax.optimization_barrier(jnp.sum(parts.astype(F32), axis=0)).astype(BF16)

    other = lax.ppermute(slab[1], "core", swap)
    pair = (slab[0].astype(F32) + other.astype(F32)).astype(BF16)
    part = total(exchange(pair.reshape(tiles, quarter, 128), "dp"))
    piece = total(exchange(part.reshape(chips, pairs, 2, 128), "chip"))

    repeated = jnp.broadcast_to(piece[None], (chips, pairs, 2, 128))
    moved = moved.reshape(chips, moved_pairs, 2, 128)
    parts = exchange(jnp.concatenate([repeated, moved], axis=1), "chip")
    part, own_rows = lax.optimization_barrier((parts[:, :pairs], parts[:, pairs:]))
    part = jnp.broadcast_to(part.reshape(1, quarter, 128), (tiles, quarter, 128))
    own = exchange(part, "dp").reshape(half, 128)
    own_rows = own_rows.reshape(2 * length, 128)
    other = lax.ppermute(jnp.concatenate([own, own_rows], axis=0), "core", swap)

    square = jax.ShapeDtypeStruct((width, width), F32)
    line = jax.ShapeDtypeStruct((1, width), F32)
    outs = pl.pallas_call(
        functools.partial(unpack_kernel, share),
        out_shape=(
            jax.ShapeDtypeStruct((length, width), BF16),
            jax.ShapeDtypeStruct(w_ctx.shape, F32),
        )
        + (square,) * 5
        + (line, line, jax.ShapeDtypeStruct((1, 1), F32)),
        in_specs=[smem] + [vmem] * 3,
        out_specs=(vmem,) * 10,
        compiler_params=params,
        name="unpack",
    )(core, own, own_rows, other)
    return (
        outs[0][None],
        outs[9].reshape(()),
        outs[1],
        outs[2],
        outs[3],
        outs[4],
        outs[5],
        outs[6],
        outs[7].reshape(width),
        outs[8].reshape(width),
    )


def solution(mesh):
    ranges, tiles = mesh.devices.shape
    split = jax.sharding.Mesh(
        mesh.devices.reshape(ranges // 2, 2, tiles), ("chip", "core", "dp")
    )
    placed = (
        P("dp", RANGE, None),
        P("dp", RANGE, None),
        P("dp", RANGE, None, None),
        P("dp", RANGE, None),
        P("dp", RANGE),
        P("dp", RANGE),
        P(),
        P(),
        P(),
        P(),
        P(),
        P(),
        P(),
        P(),
    )
    return jax.shard_map(
        body,
        mesh=split,
        in_specs=placed,
        out_specs=(P("dp", RANGE, None), P(), P(), P(), P(), P(), P(), P(), P(), P()),
        check_vma=False,
    )
```

```python
import functools

import jax
import jax.numpy as jnp
from jax import lax
from jax.experimental import pallas as pl
from jax.experimental.pallas import tpu as pltpu
from jax.sharding import PartitionSpec as P

HEADS = 4
RANGE = ("chip", "core")
F32 = jnp.float32
BF16 = jnp.bfloat16


def nn(a, b):
    return lax.dot_general(a, b, (((1,), (0,)), ((), ())), preferred_element_type=F32)


def nt(a, b):
    return lax.dot_general(a, b, (((1,), (1,)), ((), ())), preferred_element_type=F32)


def tn(a, b):
    return lax.dot_general(a, b, (((0,), (0,)), ((), ())), preferred_element_type=F32)


def hold_kernel(table_ref, out_ref):
    out_ref[...] = table_ref[...]


def pick_kernel(core_ref, idx_ref, own_ref, other_ref, out_ref):
    asks, lanes = idx_ref.shape
    rows = out_ref.shape[0]
    cap = rows // asks
    line = lax.broadcasted_iota(jnp.int32, (rows, asks), 0)
    spread = (line // cap == lax.broadcasted_iota(jnp.int32, (rows, asks), 1)).astype(BF16)
    ids = nn(spread, idx_ref[...].astype(F32).astype(BF16))
    own = lax.broadcasted_iota(jnp.int32, (rows, lanes), 0) % cap == lax.broadcasted_iota(
        jnp.int32, (rows, lanes), 1
    )
    ids = jnp.sum(jnp.where(own, ids, 0.0), axis=1, keepdims=True).astype(jnp.int32)
    hot = ids == lax.broadcasted_iota(jnp.int32, (rows, own_ref.shape[0]), 1)
    mine = lax.broadcasted_iota(jnp.int32, hot.shape, 0) // cap % 2 == core_ref[0]
    out_ref[...] = (
        nn((hot & mine).astype(BF16), own_ref[...])
        + nn((hot & ~mine).astype(BF16), other_ref[...])
    ).astype(BF16)


def step_kernel(
    node_total,
    share,
    core_ref,
    feats_ref,
    buf_ref,
    slot_ref,
    label_ref,
    relay_ref,
    w_ctx_ref,
    w_query_ref,
    w_key_ref,
    w_value_ref,
    w_proj_ref,
    w_logit_ref,
    gain_attn_ref,
    gain_out_ref,
    slab_ref,
    relayed_ref,
    ids_ref,
    extra_ref,
    prob_ref,
):
    length, width = feats_ref.shape
    slots = buf_ref.shape[0]
    kc = slot_ref.shape[0]
    head_width = width // HEADS

    ids_ref[0:kc, :] = slot_ref[...]
    ids_ref[kc : kc + 1, :] = label_ref[...]
    ids_ref[kc + 1 :, :] = jnp.zeros((8 - kc - 1, length), jnp.int32)
    ids = jnp.transpose(ids_ref[...])

    buf = buf_ref[...]
    slot_lane = lax.broadcasted_iota(jnp.int32, (length, slots), 1)
    contexts = []
    hidden0 = feats_ref[...].astype(F32)
    for k in range(kc):
        hot = (ids[:, k : k + 1] == slot_lane).astype(BF16)
        part = nn(hot, buf).astype(BF16)
        contexts.append(part)
        hidden0 = hidden0 + nn(part, w_ctx_ref[k * width : (k + 1) * width, :])

    gain_attn = gain_attn_ref[...]
    inv1 = lax.rsqrt(jnp.mean(hidden0 * hidden0, axis=1, keepdims=True) + 1e-06)
    unit1 = hidden0 * inv1
    normed = (unit1 * gain_attn).astype(BF16)
    queries = nn(normed, w_query_ref[...]).astype(BF16)
    key_rows = nn(normed, w_key_ref[...]).astype(BF16)
    value_rows = nn(normed, w_value_ref[...]).astype(BF16)

    lane_head = lax.broadcasted_iota(jnp.int32, (length, width), 1) // head_width
    causal = lax.broadcasted_iota(jnp.int32, (length, length), 0) >= lax.broadcasted_iota(
        jnp.int32, (length, length), 1
    )
    scale = 1.0 / head_width**0.5

    def of_head(rows, h):
        return jnp.where(lane_head == h, rows, jnp.zeros_like(rows))

    attended = jnp.zeros((length, width), F32)
    for h in range(HEADS):
        scores = nt(of_head(queries, h), key_rows) * scale
        scores = jnp.where(causal, scores, -1e30)
        expo = jnp.exp(scores - jnp.max(scores, axis=1, keepdims=True))
        prob = expo * (1.0 / jnp.sum(expo, axis=1, keepdims=True))
        prob_ref[h] = prob
        attended = attended + nn(prob.astype(BF16), of_head(value_rows, h))
    attended = attended.astype(BF16)
    hidden1 = hidden0 + nn(attended, w_proj_ref[...])

    line = lax.broadcasted_iota(jnp.int32, (2 * length, length), 0)
    place = relay_ref[...] == line // (2 * share) * share + line % share
    moved = nn(place.astype(BF16), hidden1.astype(BF16))
    line = lax.broadcasted_iota(jnp.int32, (2 * length, 128), 0)
    left = line // share % 2 == 0
    relayed_ref[...] = jnp.where(left, moved[:, :128], moved[:, 128:]).astype(BF16)

    gain_out = gain_out_ref[...]
    inv2 = lax.rsqrt(jnp.mean(hidden1 * hidden1, axis=1, keepdims=True) + 1e-06)
    unit2 = hidden1 * inv2
    normed_out = (unit2 * gain_out).astype(BF16)
    logits = nn(normed_out, w_logit_ref[...])
    symbol = lax.broadcasted_iota(jnp.int32, logits.shape, 1)
    target = symbol == ids[:, kc : kc + 1]
    logit_max = jnp.max(logits, axis=1, keepdims=True)
    expo = jnp.exp(logits - logit_max)
    total = jnp.sum(expo, axis=1, keepdims=True)
    picked = jnp.sum(jnp.where(target, logits, 0.0), axis=1, keepdims=True)
    losses = logit_max + jnp.log(total) - picked
    lane = lax.broadcasted_iota(jnp.int32, (length, 128), 1)
    own_lane = lax.broadcasted_iota(jnp.int32, (length, 128), 0) % 128 == lane
    loss = jnp.sum(jnp.where(own_lane, losses, 0.0), axis=0, keepdims=True) * (1.0 / node_total)

    g_logits = ((expo * (1.0 / total) - target.astype(F32)) * (1.0 / node_total)).astype(BF16)
    g_w_logit = tn(normed_out, g_logits).astype(BF16)
    g_normed_out = nt(g_logits, w_logit_ref[...]).astype(BF16).astype(F32)
    g_gain_out = jnp.sum(g_normed_out * unit2, axis=0, keepdims=True)
    g_unit = g_normed_out * gain_out
    g_hidden1 = inv2 * (g_unit - unit2 * jnp.mean(g_unit * unit2, axis=1, keepdims=True))
    g_rows = g_hidden1.astype(BF16)
    g_w_proj = tn(attended, g_rows).astype(BF16)
    g_attended = nt(g_rows, w_proj_ref[...]).astype(BF16)

    g_queries = jnp.zeros((length, width), F32)
    g_keys = jnp.zeros((length, width), F32)
    g_values = jnp.zeros((length, width), F32)
    for h in range(HEADS):
        prob = prob_ref[h]
        g_att_h = of_head(g_attended, h)
        g_prob = nt(g_att_h, value_rows).astype(BF16).astype(F32)
        g_values = g_values + tn(prob.astype(BF16), g_att_h)
        weighed = jnp.sum(g_prob * prob, axis=1, keepdims=True)
        g_scores = (prob * (g_prob - weighed) * scale).astype(BF16)
        g_queries = g_queries + nn(g_scores, of_head(key_rows, h))
        g_keys = g_keys + tn(g_scores, of_head(queries, h))
    g_queries = g_queries.astype(BF16)
    g_keys = g_keys.astype(BF16)
    g_values = g_values.astype(BF16)
    g_w_query = tn(normed, g_queries).astype(BF16)
    g_w_key = tn(normed, g_keys).astype(BF16)
    g_w_value = tn(normed, g_values).astype(BF16)
    g_normed = (
        nt(g_queries, w_query_ref[...])
        + nt(g_keys, w_key_ref[...])
        + nt(g_values, w_value_ref[...])
    )
    g_gain_attn = jnp.sum(g_normed * unit1, axis=0, keepdims=True)
    g_unit = g_normed * gain_attn
    g_hidden0 = g_hidden1 + inv1 * (
        g_unit - unit1 * jnp.mean(g_unit * unit1, axis=1, keepdims=True)
    )
    g_rows = g_hidden0.astype(BF16)
    half = slab_ref.shape[1]
    core = core_ref[0]

    def put(h, row, lines):
        slab_ref[(core + h) % 2, row : row + lines.shape[0], :] = lines

    for k in range(kc):
        g_w_ctx = tn(contexts[k], g_rows).astype(BF16)
        put(0, k * width, g_w_ctx[:, :128])
        put(0, (kc + k) * width, g_w_ctx[:, 128:])
    first = 2 * kc * width
    put(0, first, g_w_logit[:, :128])
    put(1, 0, g_w_logit[:, 128:])
    row = width
    for grad in (g_w_query, g_w_key, g_w_value, g_w_proj):
        put(1, row, grad[:, :128])
        put(1, row + width, grad[:, 128:])
        row += 2 * width
    extra_ref[...] = jnp.zeros_like(extra_ref)
    extra_ref[0:1, :] = g_gain_attn[:, :128]
    extra_ref[1:2, :] = g_gain_attn[:, 128:]
    extra_ref[2:3, :] = g_gain_out[:, :128]
    extra_ref[3:4, :] = g_gain_out[:, 128:]
    extra_ref[4:5, :] = loss
    used = first + width
    put(0, used, extra_ref[...].astype(BF16))
    put(0, used + 16, jnp.zeros((half - used - 16, 128), BF16))
    put(1, used, jnp.zeros((half - used, 128), BF16))


def unpack_kernel(
    share,
    core_ref,
    own_ref,
    own_rows_ref,
    other_ref,
    relayed_ref,
    ctx_ref,
    query_ref,
    key_ref,
    value_ref,
    proj_ref,
    logit_ref,
    attn_ref,
    out_ref,
    loss_ref,
):
    core = core_ref[0]
    rows = ctx_ref.shape[0]
    width = logit_ref.shape[0]
    half = own_ref.shape[0]

    def lines(h, start, count):
        mine = own_ref[start : start + count, :].astype(F32)
        theirs = other_ref[start : start + count, :].astype(F32)
        return jnp.where(core == h, mine, theirs)

    for row in range(0, rows, width):
        ctx_ref[row : row + width, :128] = lines(0, row, width)
        ctx_ref[row : row + width, 128:] = lines(0, rows + row, width)
    logit_ref[:, :128] = lines(0, 2 * rows, width)
    logit_ref[:, 128:] = lines(1, 0, width)
    row = width
    for ref in (query_ref, key_ref, value_ref, proj_ref):
        ref[:, :128] = lines(1, row, width)
        ref[:, 128:] = lines(1, row + width, width)
        row += 2 * width
    extra = lines(0, 2 * rows + width, 16)
    attn_ref[:, :128] = extra[0:1]
    attn_ref[:, 128:] = extra[1:2]
    out_ref[:, :128] = extra[2:3]
    out_ref[:, 128:] = extra[3:4]
    loss_ref[...] = jnp.sum(extra[4:5], axis=1, keepdims=True)

    length = relayed_ref.shape[0]
    row = lax.broadcasted_iota(jnp.int32, (length, 2 * length), 0)
    line = lax.broadcasted_iota(jnp.int32, (length, 2 * length), 1)
    mine = row // share % 2 == core
    own_rows = own_rows_ref[...]
    other_rows = other_ref[half:, :]
    for h in range(2):
        found = line == (row // (2 * share) * 4 + 2 * core + h) * share + row % share
        here = (found & mine).astype(BF16)
        there = (found & ~mine).astype(BF16)
        relayed_ref[:, h * 128 : (h + 1) * 128] = (
            nn(here, own_rows) + nn(there, other_rows)
        ).astype(BF16)


def body(
    node_feats,
    ctx_table,
    fetch_rows,
    ctx_slot,
    labels,
    relay_slot,
    w_ctx,
    w_query,
    w_key,
    w_value,
    w_proj,
    w_logit,
    gain_attn,
    gain_out,
):
    features = node_feats[0]
    length, width = features.shape
    chips, ranges = lax.axis_size("chip"), lax.axis_size(RANGE)
    table = ctx_table[0]
    requests = fetch_rows[0, 0]
    cap = requests.shape[1]
    tiles = lax.axis_size("dp")
    share = length // ranges
    core = lax.axis_index("core").astype(jnp.int32).reshape(1)
    half = (w_ctx.shape[0] * width + 5 * width * width) // 256 + 16
    half = -(-half // (2 * tiles * chips)) * (2 * tiles * chips)
    quarter = half // tiles
    pairs = quarter // (2 * chips)
    moved_pairs = length // chips
    swap = [(0, 1), (1, 0)]
    vmem = pl.BlockSpec(memory_space=pltpu.VMEM)
    params = pltpu.CompilerParams(vmem_limit_bytes=32 * 1024 * 1024)

    smem = pl.BlockSpec(memory_space=pltpu.SMEM)

    def exchange(lines, axis):
        return lax.all_to_all(lines, axis, split_axis=0, concat_axis=0, tiled=True)

    asks = jnp.pad(requests, ((0, 0), (0, 128 - cap))).reshape(chips, 2, 128)
    asked = exchange(asks, "chip")
    held = pl.pallas_call(
        hold_kernel,
        out_shape=jax.ShapeDtypeStruct(table.shape, BF16),
        in_specs=[vmem],
        out_specs=vmem,
        compiler_params=params,
        cost_estimate=pl.CostEstimate(flops=0, bytes_accessed=131072, transcendentals=0),
        name="hold_table",
    )(table)
    other_table = lax.ppermute(held, "core", swap)
    picked = pl.pallas_call(
        pick_kernel,
        out_shape=jax.ShapeDtypeStruct((ranges * cap, width), BF16),
        in_specs=[smem] + [vmem] * 3,
        out_specs=vmem,
        compiler_params=params,
        name="pick_rows",
    )(core, asked.reshape(ranges, 128), held, other_table)
    buffer = exchange(picked.reshape(chips, 2 * cap, width), "chip").reshape(ranges * cap, width)

    slab, moved = pl.pallas_call(
        functools.partial(step_kernel, float(length * ranges * tiles), share),
        out_shape=(
            jax.ShapeDtypeStruct((2, half, 128), BF16),
            jax.ShapeDtypeStruct((2 * length, 128), BF16),
        ),
        in_specs=[smem] + [vmem] * 13,
        out_specs=(vmem, vmem),
        scratch_shapes=[
            pltpu.VMEM((8, length), jnp.int32),
            pltpu.VMEM((16, 128), F32),
            pltpu.VMEM((HEADS, length, length), F32),
        ],
        compiler_params=params,
        name="window_step",
    )(
        core,
        features,
        buffer,
        jnp.transpose(ctx_slot[0]),
        labels,
        relay_slot,
        w_ctx,
        w_query,
        w_key,
        w_value,
        w_proj,
        w_logit,
        gain_attn.reshape(1, width),
        gain_out.reshape(1, width),
    )

    def total(parts):
        return lax.optimization_barrier(jnp.sum(parts.astype(F32), axis=0)).astype(BF16)

    other = lax.ppermute(slab[1], "core", swap)
    pair = (slab[0].astype(F32) + other.astype(F32)).astype(BF16)
    part = total(exchange(pair.reshape(tiles, quarter, 128), "dp"))
    piece = total(exchange(part.reshape(chips, pairs, 2, 128), "chip"))

    repeated = jnp.broadcast_to(piece[None], (chips, pairs, 2, 128))
    moved = moved.reshape(chips, moved_pairs, 2, 128)
    parts = exchange(jnp.concatenate([repeated, moved], axis=1), "chip")
    part, own_rows = lax.optimization_barrier((parts[:, :pairs], parts[:, pairs:]))
    part = jnp.broadcast_to(part.reshape(1, quarter, 128), (tiles, quarter, 128))
    own = exchange(part, "dp").reshape(half, 128)
    own_rows = own_rows.reshape(2 * length, 128)
    other = lax.ppermute(jnp.concatenate([own, own_rows], axis=0), "core", swap)

    square = jax.ShapeDtypeStruct((width, width), F32)
    line = jax.ShapeDtypeStruct((1, width), F32)
    outs = pl.pallas_call(
        functools.partial(unpack_kernel, share),
        out_shape=(
            jax.ShapeDtypeStruct((length, width), BF16),
            jax.ShapeDtypeStruct(w_ctx.shape, F32),
        )
        + (square,) * 5
        + (line, line, jax.ShapeDtypeStruct((1, 1), F32)),
        in_specs=[smem] + [vmem] * 3,
        out_specs=(vmem,) * 10,
        compiler_params=params,
        name="unpack",
    )(core, own, own_rows, other)
    return (
        outs[0][None],
        outs[9].reshape(()),
        outs[1],
        outs[2],
        outs[3],
        outs[4],
        outs[5],
        outs[6],
        outs[7].reshape(width),
        outs[8].reshape(width),
    )


def solution(mesh):
    ranges, tiles = mesh.devices.shape
    split = jax.sharding.Mesh(
        mesh.devices.reshape(ranges // 2, 2, tiles), ("chip", "core", "dp")
    )
    placed = (
        P("dp", RANGE, None),
        P("dp", RANGE, None),
        P("dp", RANGE, None, None),
        P("dp", RANGE, None),
        P("dp", RANGE),
        P("dp", RANGE),
        P(),
        P(),
        P(),
        P(),
        P(),
        P(),
        P(),
        P(),
    )
    return jax.shard_map(
        body,
        mesh=split,
        in_specs=placed,
        out_specs=(P("dp", RANGE, None), P(), P(), P(), P(), P(), P(), P(), P(), P()),
        check_vma=False,
    )
```

```python
import functools

import jax
import jax.numpy as jnp
from jax import lax
from jax.experimental import pallas as pl
from jax.experimental.pallas import tpu as pltpu
from jax.sharding import PartitionSpec as P

HEADS = 4
RANGE = ("chip", "core")
F32 = jnp.float32
BF16 = jnp.bfloat16


def nn(a, b):
    return lax.dot_general(a, b, (((1,), (0,)), ((), ())), preferred_element_type=F32)


def nt(a, b):
    return lax.dot_general(a, b, (((1,), (1,)), ((), ())), preferred_element_type=F32)


def tn(a, b):
    return lax.dot_general(a, b, (((0,), (0,)), ((), ())), preferred_element_type=F32)


def hold_kernel(table_ref, out_ref):
    out_ref[...] = table_ref[...]


def pick_kernel(core_ref, idx_ref, own_ref, other_ref, out_ref):
    asks, lanes = idx_ref.shape
    rows = out_ref.shape[0]
    cap = rows // asks
    line = lax.broadcasted_iota(jnp.int32, (rows, asks), 0)
    spread = (line // cap == lax.broadcasted_iota(jnp.int32, (rows, asks), 1)).astype(BF16)
    ids = nn(spread, idx_ref[...].astype(F32).astype(BF16))
    own = lax.broadcasted_iota(jnp.int32, (rows, lanes), 0) % cap == lax.broadcasted_iota(
        jnp.int32, (rows, lanes), 1
    )
    ids = jnp.sum(jnp.where(own, ids, 0.0), axis=1, keepdims=True).astype(jnp.int32)
    hot = ids == lax.broadcasted_iota(jnp.int32, (rows, own_ref.shape[0]), 1)
    mine = lax.broadcasted_iota(jnp.int32, hot.shape, 0) // cap % 2 == core_ref[0]
    out_ref[...] = (
        nn((hot & mine).astype(BF16), own_ref[...])
        + nn((hot & ~mine).astype(BF16), other_ref[...])
    ).astype(BF16)


def step_kernel(
    node_total,
    share,
    core_ref,
    feats_ref,
    buf_ref,
    slot_ref,
    label_ref,
    relay_ref,
    w_ctx_ref,
    w_query_ref,
    w_key_ref,
    w_value_ref,
    w_proj_ref,
    w_logit_ref,
    gain_attn_ref,
    gain_out_ref,
    slab_ref,
    relayed_ref,
    ids_ref,
    extra_ref,
    prob_ref,
):
    length, width = feats_ref.shape
    slots = buf_ref.shape[0]
    kc = slot_ref.shape[0]
    head_width = width // HEADS

    ids_ref[0:kc, :] = slot_ref[...]
    ids_ref[kc : kc + 1, :] = label_ref[...]
    ids_ref[kc + 1 :, :] = jnp.zeros((8 - kc - 1, length), jnp.int32)
    ids = jnp.transpose(ids_ref[...])

    buf = buf_ref[...]
    slot_lane = lax.broadcasted_iota(jnp.int32, (length, slots), 1)
    contexts = []
    hidden0 = feats_ref[...].astype(F32)
    for k in range(kc):
        hot = (ids[:, k : k + 1] == slot_lane).astype(BF16)
        part = nn(hot, buf).astype(BF16)
        contexts.append(part)
        hidden0 = hidden0 + nn(part, w_ctx_ref[k * width : (k + 1) * width, :])

    gain_attn = gain_attn_ref[...]
    inv1 = lax.rsqrt(jnp.mean(hidden0 * hidden0, axis=1, keepdims=True) + 1e-06)
    unit1 = hidden0 * inv1
    normed = (unit1 * gain_attn).astype(BF16)
    queries = nn(normed, w_query_ref[...]).astype(BF16)
    key_rows = nn(normed, w_key_ref[...]).astype(BF16)
    value_rows = nn(normed, w_value_ref[...]).astype(BF16)

    lane_head = lax.broadcasted_iota(jnp.int32, (length, width), 1) // head_width
    causal = lax.broadcasted_iota(jnp.int32, (length, length), 0) >= lax.broadcasted_iota(
        jnp.int32, (length, length), 1
    )
    scale = 1.0 / head_width**0.5

    def of_head(rows, h):
        return jnp.where(lane_head == h, rows, jnp.zeros_like(rows))

    attended = jnp.zeros((length, width), F32)
    for h in range(HEADS):
        scores = nt(of_head(queries, h), key_rows) * scale
        scores = jnp.where(causal, scores, -1e30)
        expo = jnp.exp(scores - jnp.max(scores, axis=1, keepdims=True))
        prob = expo * (1.0 / jnp.sum(expo, axis=1, keepdims=True))
        prob_ref[h] = prob
        attended = attended + nn(prob.astype(BF16), of_head(value_rows, h))
    attended = attended.astype(BF16)
    hidden1 = hidden0 + nn(attended, w_proj_ref[...])

    line = lax.broadcasted_iota(jnp.int32, (2 * length, length), 0)
    place = relay_ref[...] == line // (2 * share) * share + line % share
    moved = nn(place.astype(BF16), hidden1.astype(BF16))
    line = lax.broadcasted_iota(jnp.int32, (2 * length, 128), 0)
    left = line // share % 2 == 0
    relayed_ref[...] = jnp.where(left, moved[:, :128], moved[:, 128:]).astype(BF16)

    gain_out = gain_out_ref[...]
    inv2 = lax.rsqrt(jnp.mean(hidden1 * hidden1, axis=1, keepdims=True) + 1e-06)
    unit2 = hidden1 * inv2
    normed_out = (unit2 * gain_out).astype(BF16)
    logits = nn(normed_out, w_logit_ref[...])
    symbol = lax.broadcasted_iota(jnp.int32, logits.shape, 1)
    target = symbol == ids[:, kc : kc + 1]
    logit_max = jnp.max(logits, axis=1, keepdims=True)
    expo = jnp.exp(logits - logit_max)
    total = jnp.sum(expo, axis=1, keepdims=True)
    picked = jnp.sum(jnp.where(target, logits, 0.0), axis=1, keepdims=True)
    losses = logit_max + jnp.log(total) - picked
    lane = lax.broadcasted_iota(jnp.int32, (length, 128), 1)
    own_lane = lax.broadcasted_iota(jnp.int32, (length, 128), 0) % 128 == lane
    loss = jnp.sum(jnp.where(own_lane, losses, 0.0), axis=0, keepdims=True) * (1.0 / node_total)

    g_logits = ((expo * (1.0 / total) - target.astype(F32)) * (1.0 / node_total)).astype(BF16)
    g_w_logit = tn(normed_out, g_logits).astype(BF16)
    g_normed_out = nt(g_logits, w_logit_ref[...]).astype(BF16).astype(F32)
    g_gain_out = jnp.sum(g_normed_out * unit2, axis=0, keepdims=True)
    g_unit = g_normed_out * gain_out
    g_hidden1 = inv2 * (g_unit - unit2 * jnp.mean(g_unit * unit2, axis=1, keepdims=True))
    g_rows = g_hidden1.astype(BF16)
    g_w_proj = tn(attended, g_rows).astype(BF16)
    g_attended = nt(g_rows, w_proj_ref[...]).astype(BF16)

    g_queries = jnp.zeros((length, width), F32)
    g_keys = jnp.zeros((length, width), F32)
    g_values = jnp.zeros((length, width), F32)
    for h in range(HEADS):
        prob = prob_ref[h]
        g_att_h = of_head(g_attended, h)
        g_prob = nt(g_att_h, value_rows).astype(BF16).astype(F32)
        g_values = g_values + tn(prob.astype(BF16), g_att_h)
        weighed = jnp.sum(g_prob * prob, axis=1, keepdims=True)
        g_scores = (prob * (g_prob - weighed) * scale).astype(BF16)
        g_queries = g_queries + nn(g_scores, of_head(key_rows, h))
        g_keys = g_keys + tn(g_scores, of_head(queries, h))
    g_queries = g_queries.astype(BF16)
    g_keys = g_keys.astype(BF16)
    g_values = g_values.astype(BF16)
    g_w_query = tn(normed, g_queries).astype(BF16)
    g_w_key = tn(normed, g_keys).astype(BF16)
    g_w_value = tn(normed, g_values).astype(BF16)
    g_normed = (
        nt(g_queries, w_query_ref[...])
        + nt(g_keys, w_key_ref[...])
        + nt(g_values, w_value_ref[...])
    )
    g_gain_attn = jnp.sum(g_normed * unit1, axis=0, keepdims=True)
    g_unit = g_normed * gain_attn
    g_hidden0 = g_hidden1 + inv1 * (
        g_unit - unit1 * jnp.mean(g_unit * unit1, axis=1, keepdims=True)
    )
    g_rows = g_hidden0.astype(BF16)
    half = slab_ref.shape[1]
    core = core_ref[0]

    def put(h, row, lines):
        slab_ref[(core + h) % 2, row : row + lines.shape[0], :] = lines

    for k in range(kc):
        g_w_ctx = tn(contexts[k], g_rows).astype(BF16)
        put(0, k * width, g_w_ctx[:, :128])
        put(0, (kc + k) * width, g_w_ctx[:, 128:])
    first = 2 * kc * width
    put(0, first, g_w_logit[:, :128])
    put(1, 0, g_w_logit[:, 128:])
    row = width
    for grad in (g_w_query, g_w_key, g_w_value, g_w_proj):
        put(1, row, grad[:, :128])
        put(1, row + width, grad[:, 128:])
        row += 2 * width
    extra_ref[...] = jnp.zeros_like(extra_ref)
    extra_ref[0:1, :] = g_gain_attn[:, :128]
    extra_ref[1:2, :] = g_gain_attn[:, 128:]
    extra_ref[2:3, :] = g_gain_out[:, :128]
    extra_ref[3:4, :] = g_gain_out[:, 128:]
    extra_ref[4:5, :] = loss
    used = first + width
    put(0, used, extra_ref[...].astype(BF16))
    put(0, used + 16, jnp.zeros((half - used - 16, 128), BF16))
    put(1, used, jnp.zeros((half - used, 128), BF16))


def unpack_kernel(
    share,
    core_ref,
    own_ref,
    own_rows_ref,
    other_ref,
    relayed_ref,
    ctx_ref,
    query_ref,
    key_ref,
    value_ref,
    proj_ref,
    logit_ref,
    attn_ref,
    out_ref,
    loss_ref,
    wide_ref,
    sems,
):
    core = core_ref[0]
    rows = ctx_ref.shape[0]
    width = logit_ref.shape[0]
    half = own_ref.shape[0]

    def lines(h, start, count):
        mine = own_ref[start : start + count, :].astype(F32)
        theirs = other_ref[start : start + count, :].astype(F32)
        return jnp.where(core == h, mine, theirs)

    copies = []

    def leave(target, left, right):
        n = len(copies)
        block = wide_ref.at[n * width : (n + 1) * width, :]
        block[:, :128] = left
        block[:, 128:] = right
        copies.append(pltpu.make_async_copy(block, target, sems.at[n]))
        copies[n].start()

    for row in range(0, rows, width):
        target = ctx_ref.at[row : row + width, :]
        leave(target, lines(0, row, width), lines(0, rows + row, width))
    leave(logit_ref, lines(0, 2 * rows, width), lines(1, 0, width))
    row = width
    for ref in (query_ref, key_ref, value_ref, proj_ref):
        leave(ref, lines(1, row, width), lines(1, row + width, width))
        row += 2 * width
    extra = lines(0, 2 * rows + width, 16)
    attn_ref[:, :128] = extra[0:1]
    attn_ref[:, 128:] = extra[1:2]
    out_ref[:, :128] = extra[2:3]
    out_ref[:, 128:] = extra[3:4]
    loss_ref[...] = jnp.sum(extra[4:5], axis=1, keepdims=True)

    length = relayed_ref.shape[0]
    row = lax.broadcasted_iota(jnp.int32, (length, 2 * length), 0)
    line = lax.broadcasted_iota(jnp.int32, (length, 2 * length), 1)
    mine = row // share % 2 == core
    own_rows = own_rows_ref[...]
    other_rows = other_ref[half:, :]
    for h in range(2):
        found = line == (row // (2 * share) * 4 + 2 * core + h) * share + row % share
        here = (found & mine).astype(BF16)
        there = (found & ~mine).astype(BF16)
        relayed_ref[:, h * 128 : (h + 1) * 128] = (
            nn(here, own_rows) + nn(there, other_rows)
        ).astype(BF16)
    for copy in copies:
        copy.wait()


def body(
    node_feats,
    ctx_table,
    fetch_rows,
    ctx_slot,
    labels,
    relay_slot,
    w_ctx,
    w_query,
    w_key,
    w_value,
    w_proj,
    w_logit,
    gain_attn,
    gain_out,
):
    features = node_feats[0]
    length, width = features.shape
    chips, ranges = lax.axis_size("chip"), lax.axis_size(RANGE)
    table = ctx_table[0]
    requests = fetch_rows[0, 0]
    cap = requests.shape[1]
    tiles = lax.axis_size("dp")
    share = length // ranges
    core = lax.axis_index("core").astype(jnp.int32).reshape(1)
    half = (w_ctx.shape[0] * width + 5 * width * width) // 256 + 16
    half = -(-half // (2 * tiles * chips)) * (2 * tiles * chips)
    quarter = half // tiles
    pairs = quarter // (2 * chips)
    moved_pairs = length // chips
    swap = [(0, 1), (1, 0)]
    vmem = pl.BlockSpec(memory_space=pltpu.VMEM)
    params = pltpu.CompilerParams(vmem_limit_bytes=32 * 1024 * 1024)

    smem = pl.BlockSpec(memory_space=pltpu.SMEM)

    def exchange(lines, axis):
        return lax.all_to_all(lines, axis, split_axis=0, concat_axis=0, tiled=True)

    asks = jnp.pad(requests, ((0, 0), (0, 128 - cap))).reshape(chips, 2, 128)
    asked = exchange(asks, "chip")
    held = pl.pallas_call(
        hold_kernel,
        out_shape=jax.ShapeDtypeStruct(table.shape, BF16),
        in_specs=[vmem],
        out_specs=vmem,
        compiler_params=params,
        cost_estimate=pl.CostEstimate(flops=0, bytes_accessed=131072, transcendentals=0),
        name="hold_table",
    )(table)
    other_table = lax.ppermute(held, "core", swap)
    picked = pl.pallas_call(
        pick_kernel,
        out_shape=jax.ShapeDtypeStruct((ranges * cap, width), BF16),
        in_specs=[smem] + [vmem] * 3,
        out_specs=vmem,
        compiler_params=params,
        name="pick_rows",
    )(core, asked.reshape(ranges, 128), held, other_table)
    buffer = exchange(picked.reshape(chips, 2 * cap, width), "chip").reshape(ranges * cap, width)

    slab, moved = pl.pallas_call(
        functools.partial(step_kernel, float(length * ranges * tiles), share),
        out_shape=(
            jax.ShapeDtypeStruct((2, half, 128), BF16),
            jax.ShapeDtypeStruct((2 * length, 128), BF16),
        ),
        in_specs=[smem] + [vmem] * 13,
        out_specs=(vmem, vmem),
        scratch_shapes=[
            pltpu.VMEM((8, length), jnp.int32),
            pltpu.VMEM((16, 128), F32),
            pltpu.VMEM((HEADS, length, length), F32),
        ],
        compiler_params=params,
        name="window_step",
    )(
        core,
        features,
        buffer,
        jnp.transpose(ctx_slot[0]),
        labels,
        relay_slot,
        w_ctx,
        w_query,
        w_key,
        w_value,
        w_proj,
        w_logit,
        gain_attn.reshape(1, width),
        gain_out.reshape(1, width),
    )

    def total(parts):
        return lax.optimization_barrier(jnp.sum(parts.astype(F32), axis=0)).astype(BF16)

    other = lax.ppermute(slab[1], "core", swap)
    pair = (slab[0].astype(F32) + other.astype(F32)).astype(BF16)
    part = total(exchange(pair.reshape(tiles, quarter, 128), "dp"))
    piece = total(exchange(part.reshape(chips, pairs, 2, 128), "chip"))

    repeated = jnp.broadcast_to(piece[None], (chips, pairs, 2, 128))
    moved = moved.reshape(chips, moved_pairs, 2, 128)
    parts = exchange(jnp.concatenate([repeated, moved], axis=1), "chip")
    part, own_rows = lax.optimization_barrier((parts[:, :pairs], parts[:, pairs:]))
    part = jnp.broadcast_to(part.reshape(1, quarter, 128), (tiles, quarter, 128))
    own = exchange(part, "dp").reshape(half, 128)
    own_rows = own_rows.reshape(2 * length, 128)
    other = lax.ppermute(jnp.concatenate([own, own_rows], axis=0), "core", swap)

    square = jax.ShapeDtypeStruct((width, width), F32)
    line = jax.ShapeDtypeStruct((1, width), F32)
    outs = pl.pallas_call(
        functools.partial(unpack_kernel, share),
        out_shape=(
            jax.ShapeDtypeStruct((length, width), BF16),
            jax.ShapeDtypeStruct(w_ctx.shape, F32),
        )
        + (square,) * 5
        + (line, line, jax.ShapeDtypeStruct((1, 1), F32)),
        in_specs=[smem] + [vmem] * 3,
        out_specs=(vmem,) + (pl.BlockSpec(memory_space=pl.ANY),) * 6 + (vmem,) * 3,
        scratch_shapes=[
            pltpu.VMEM((w_ctx.shape[0] + 5 * width, width), F32),
            pltpu.SemaphoreType.DMA((w_ctx.shape[0] // width + 5,)),
        ],
        compiler_params=params,
        name="unpack",
    )(core, own, own_rows, other)
    return (
        outs[0][None],
        outs[9].reshape(()),
        outs[1],
        outs[2],
        outs[3],
        outs[4],
        outs[5],
        outs[6],
        outs[7].reshape(width),
        outs[8].reshape(width),
    )


def solution(mesh):
    ranges, tiles = mesh.devices.shape
    split = jax.sharding.Mesh(
        mesh.devices.reshape(ranges // 2, 2, tiles), ("chip", "core", "dp")
    )
    placed = (
        P("dp", RANGE, None),
        P("dp", RANGE, None),
        P("dp", RANGE, None, None),
        P("dp", RANGE, None),
        P("dp", RANGE),
        P("dp", RANGE),
        P(),
        P(),
        P(),
        P(),
        P(),
        P(),
        P(),
        P(),
    )
    return jax.shard_map(
        body,
        mesh=split,
        in_specs=placed,
        out_specs=(P("dp", RANGE, None), P(), P(), P(), P(), P(), P(), P(), P(), P()),
        check_vma=False,
    )
```

```python
import functools

import jax
import jax.numpy as jnp
from jax import lax
from jax.experimental import pallas as pl
from jax.experimental.pallas import tpu as pltpu
from jax.sharding import PartitionSpec as P

HEADS = 4
RANGE = ("chip", "core")
F32 = jnp.float32
BF16 = jnp.bfloat16


def nn(a, b):
    return lax.dot_general(a, b, (((1,), (0,)), ((), ())), preferred_element_type=F32)


def nt(a, b):
    return lax.dot_general(a, b, (((1,), (1,)), ((), ())), preferred_element_type=F32)


def tn(a, b):
    return lax.dot_general(a, b, (((0,), (0,)), ((), ())), preferred_element_type=F32)


def ask_kernel(asks_ref, table_ref, out_ref, held_ref):
    cap, owners = asks_ref.shape
    lines = jnp.concatenate([asks_ref[...], jnp.zeros((128 - cap, owners), jnp.int32)], axis=0)
    out_ref[...] = jnp.transpose(lines).astype(F32).astype(BF16)
    held_ref[...] = table_ref[...]


def pick_kernel(core_ref, idx_ref, own_ref, other_ref, out_ref):
    asks, lanes = idx_ref.shape
    rows = out_ref.shape[0]
    cap = rows // asks
    line = lax.broadcasted_iota(jnp.int32, (rows, asks), 0)
    spread = (line // cap == lax.broadcasted_iota(jnp.int32, (rows, asks), 1)).astype(BF16)
    ids = nn(spread, idx_ref[...])
    own = lax.broadcasted_iota(jnp.int32, (rows, lanes), 0) % cap == lax.broadcasted_iota(
        jnp.int32, (rows, lanes), 1
    )
    ids = jnp.sum(jnp.where(own, ids, 0.0), axis=1, keepdims=True).astype(jnp.int32)
    hot = ids == lax.broadcasted_iota(jnp.int32, (rows, own_ref.shape[0]), 1)
    mine = lax.broadcasted_iota(jnp.int32, hot.shape, 0) // cap % 2 == core_ref[0]
    out_ref[...] = (
        nn((hot & mine).astype(BF16), own_ref[...])
        + nn((hot & ~mine).astype(BF16), other_ref[...])
    ).astype(BF16)


def step_kernel(
    node_total,
    share,
    core_ref,
    feats_ref,
    buf_ref,
    slot_ref,
    label_ref,
    relay_ref,
    w_ctx_ref,
    w_query_ref,
    w_key_ref,
    w_value_ref,
    w_proj_ref,
    w_logit_ref,
    gain_attn_ref,
    gain_out_ref,
    slab_ref,
    relayed_ref,
    ids_ref,
    extra_ref,
    prob_ref,
):
    length, width = feats_ref.shape
    slots = buf_ref.shape[0]
    kc = slot_ref.shape[0]
    head_width = width // HEADS

    ids_ref[0:kc, :] = slot_ref[...]
    ids_ref[kc : kc + 1, :] = label_ref[...]
    ids_ref[kc + 1 :, :] = jnp.zeros((8 - kc - 1, length), jnp.int32)
    ids = jnp.transpose(ids_ref[...])

    buf = buf_ref[...]
    slot_lane = lax.broadcasted_iota(jnp.int32, (length, slots), 1)
    contexts = []
    hidden0 = feats_ref[...].astype(F32)
    for k in range(kc):
        hot = (ids[:, k : k + 1] == slot_lane).astype(BF16)
        part = nn(hot, buf).astype(BF16)
        contexts.append(part)
        hidden0 = hidden0 + nn(part, w_ctx_ref[k * width : (k + 1) * width, :])

    gain_attn = gain_attn_ref[...]
    inv1 = lax.rsqrt(jnp.mean(hidden0 * hidden0, axis=1, keepdims=True) + 1e-06)
    unit1 = hidden0 * inv1
    normed = (unit1 * gain_attn).astype(BF16)
    queries = nn(normed, w_query_ref[...]).astype(BF16)
    key_rows = nn(normed, w_key_ref[...]).astype(BF16)
    value_rows = nn(normed, w_value_ref[...]).astype(BF16)

    lane_head = lax.broadcasted_iota(jnp.int32, (length, width), 1) // head_width
    causal = lax.broadcasted_iota(jnp.int32, (length, length), 0) >= lax.broadcasted_iota(
        jnp.int32, (length, length), 1
    )
    scale = 1.0 / head_width**0.5

    def of_head(rows, h):
        return jnp.where(lane_head == h, rows, jnp.zeros_like(rows))

    attended = jnp.zeros((length, width), F32)
    for h in range(HEADS):
        scores = nt(of_head(queries, h), key_rows) * scale
        scores = jnp.where(causal, scores, -1e30)
        expo = jnp.exp(scores - jnp.max(scores, axis=1, keepdims=True))
        prob = expo / jnp.sum(expo, axis=1, keepdims=True)
        prob_ref[h] = prob
        attended = attended + nn(prob.astype(BF16), of_head(value_rows, h))
    attended = attended.astype(BF16)
    hidden1 = hidden0 + nn(attended, w_proj_ref[...])

    line = lax.broadcasted_iota(jnp.int32, (2 * length, length), 0)
    place = relay_ref[...] == line // (2 * share) * share + line % share
    moved = nn(place.astype(BF16), hidden1.astype(BF16))
    line = lax.broadcasted_iota(jnp.int32, (2 * length, 128), 0)
    left = line // share % 2 == 0
    relayed_ref[...] = jnp.where(left, moved[:, :128], moved[:, 128:]).astype(BF16)

    gain_out = gain_out_ref[...]
    inv2 = lax.rsqrt(jnp.mean(hidden1 * hidden1, axis=1, keepdims=True) + 1e-06)
    unit2 = hidden1 * inv2
    normed_out = (unit2 * gain_out).astype(BF16)
    logits = nn(normed_out, w_logit_ref[...])
    symbol = lax.broadcasted_iota(jnp.int32, logits.shape, 1)
    target = symbol == ids[:, kc : kc + 1]
    logit_max = jnp.max(logits, axis=1, keepdims=True)
    expo = jnp.exp(logits - logit_max)
    total = jnp.sum(expo, axis=1, keepdims=True)
    picked = jnp.sum(jnp.where(target, logits, 0.0), axis=1, keepdims=True)
    losses = logit_max + jnp.log(total) - picked
    lane = lax.broadcasted_iota(jnp.int32, (length, 128), 1)
    own_lane = lax.broadcasted_iota(jnp.int32, (length, 128), 0) % 128 == lane
    loss = jnp.sum(jnp.where(own_lane, losses, 0.0), axis=0, keepdims=True) * (1.0 / node_total)

    g_logits = ((expo / total - target.astype(F32)) * (1.0 / node_total)).astype(BF16)
    g_w_logit = tn(normed_out, g_logits).astype(BF16)
    g_normed_out = nt(g_logits, w_logit_ref[...]).astype(BF16).astype(F32)
    g_gain_out = jnp.sum(g_normed_out * unit2, axis=0, keepdims=True)
    g_unit = g_normed_out * gain_out
    g_hidden1 = inv2 * (g_unit - unit2 * jnp.mean(g_unit * unit2, axis=1, keepdims=True))
    g_rows = g_hidden1.astype(BF16)
    g_w_proj = tn(attended, g_rows).astype(BF16)
    g_attended = nt(g_rows, w_proj_ref[...]).astype(BF16)

    g_queries = jnp.zeros((length, width), F32)
    g_keys = jnp.zeros((length, width), F32)
    g_values = jnp.zeros((length, width), F32)
    for h in range(HEADS):
        prob = prob_ref[h]
        g_att_h = of_head(g_attended, h)
        g_prob = nt(g_att_h, value_rows).astype(BF16).astype(F32)
        g_values = g_values + tn(prob.astype(BF16), g_att_h)
        weighed = jnp.sum(g_prob * prob, axis=1, keepdims=True)
        g_scores = (prob * (g_prob - weighed) * scale).astype(BF16)
        g_queries = g_queries + nn(g_scores, of_head(key_rows, h))
        g_keys = g_keys + tn(g_scores, of_head(queries, h))
    g_queries = g_queries.astype(BF16)
    g_keys = g_keys.astype(BF16)
    g_values = g_values.astype(BF16)
    g_qkv = jnp.concatenate([g_queries, g_keys, g_values], axis=1)
    g_w_qkv = tn(normed, g_qkv).astype(BF16)
    g_w_query, g_w_key, g_w_value = (g_w_qkv[:, i * width : (i + 1) * width] for i in range(3))
    g_normed = (
        nt(g_queries, w_query_ref[...])
        + nt(g_keys, w_key_ref[...])
        + nt(g_values, w_value_ref[...])
    )
    g_gain_attn = jnp.sum(g_normed * unit1, axis=0, keepdims=True)
    g_unit = g_normed * gain_attn
    g_hidden0 = g_hidden1 + inv1 * (
        g_unit - unit1 * jnp.mean(g_unit * unit1, axis=1, keepdims=True)
    )
    g_rows = g_hidden0.astype(BF16)
    half = slab_ref.shape[1]
    core = core_ref[0]

    def put(h, row, lines):
        slab_ref[(core + h) % 2, row : row + lines.shape[0], :] = lines

    for k in range(kc):
        g_w_ctx = tn(contexts[k], g_rows).astype(BF16)
        put(0, k * width, g_w_ctx[:, :128])
        put(0, (kc + k) * width, g_w_ctx[:, 128:])
    first = 2 * kc * width
    put(0, first, g_w_logit[:, :128])
    put(1, 0, g_w_logit[:, 128:])
    row = width
    for grad in (g_w_query, g_w_key, g_w_value, g_w_proj):
        put(1, row, grad[:, :128])
        put(1, row + width, grad[:, 128:])
        row += 2 * width
    extra_ref[...] = jnp.zeros_like(extra_ref)
    extra_ref[0:1, :] = g_gain_attn[:, :128]
    extra_ref[1:2, :] = g_gain_attn[:, 128:]
    extra_ref[2:3, :] = g_gain_out[:, :128]
    extra_ref[3:4, :] = g_gain_out[:, 128:]
    extra_ref[4:5, :] = loss
    used = first + width
    put(0, used, extra_ref[...].astype(BF16))
    put(0, used + 16, jnp.zeros((half - used - 16, 128), BF16))
    put(1, used, jnp.zeros((half - used, 128), BF16))


def unpack_kernel(
    share,
    core_ref,
    own_ref,
    own_rows_ref,
    other_ref,
    relayed_ref,
    ctx_ref,
    query_ref,
    key_ref,
    value_ref,
    proj_ref,
    logit_ref,
    attn_ref,
    out_ref,
    loss_ref,
):
    core = core_ref[0]
    rows = ctx_ref.shape[0]
    width = logit_ref.shape[0]
    half = own_ref.shape[0]

    def lines(h, start, count):
        mine = own_ref[start : start + count, :].astype(F32)
        theirs = other_ref[start : start + count, :].astype(F32)
        return jnp.where(core == h, mine, theirs)

    for row in range(0, rows, width):
        ctx_ref[row : row + width, :128] = lines(0, row, width)
        ctx_ref[row : row + width, 128:] = lines(0, rows + row, width)
    logit_ref[:, :128] = lines(0, 2 * rows, width)
    logit_ref[:, 128:] = lines(1, 0, width)
    row = width
    for ref in (query_ref, key_ref, value_ref, proj_ref):
        ref[:, :128] = lines(1, row, width)
        ref[:, 128:] = lines(1, row + width, width)
        row += 2 * width
    extra = lines(0, 2 * rows + width, 16)
    attn_ref[:, :128] = extra[0:1]
    attn_ref[:, 128:] = extra[1:2]
    out_ref[:, :128] = extra[2:3]
    out_ref[:, 128:] = extra[3:4]
    loss_ref[...] = jnp.sum(extra[4:5], axis=1, keepdims=True)

    length = relayed_ref.shape[0]
    row = lax.broadcasted_iota(jnp.int32, (length, 2 * length), 0)
    line = lax.broadcasted_iota(jnp.int32, (length, 2 * length), 1)
    mine = row // share % 2 == core
    own_rows = own_rows_ref[...]
    other_rows = other_ref[half:, :]
    for h in range(2):
        found = line == (row // (2 * share) * 4 + 2 * core + h) * share + row % share
        here = (found & mine).astype(BF16)
        there = (found & ~mine).astype(BF16)
        relayed_ref[:, h * 128 : (h + 1) * 128] = (
            nn(here, own_rows) + nn(there, other_rows)
        ).astype(BF16)


def body(
    node_feats,
    ctx_table,
    fetch_rows,
    ctx_slot,
    labels,
    relay_slot,
    w_ctx,
    w_query,
    w_key,
    w_value,
    w_proj,
    w_logit,
    gain_attn,
    gain_out,
):
    features = node_feats[0]
    length, width = features.shape
    chips, ranges = lax.axis_size("chip"), lax.axis_size(RANGE)
    table = ctx_table[0]
    requests = fetch_rows[0, 0]
    cap = requests.shape[1]
    tiles = lax.axis_size("dp")
    share = length // ranges
    core = lax.axis_index("core").astype(jnp.int32).reshape(1)
    half = (w_ctx.shape[0] * width + 5 * width * width) // 256 + 16
    half = -(-half // (2 * tiles * chips)) * (2 * tiles * chips)
    quarter = half // tiles
    pairs = quarter // (2 * chips)
    moved_pairs = length // chips
    swap = [(0, 1), (1, 0)]
    vmem = pl.BlockSpec(memory_space=pltpu.VMEM)
    params = pltpu.CompilerParams(vmem_limit_bytes=32 * 1024 * 1024)

    smem = pl.BlockSpec(memory_space=pltpu.SMEM)

    def exchange(lines, axis):
        return lax.all_to_all(lines, axis, split_axis=0, concat_axis=0, tiled=True)

    asks, held = pl.pallas_call(
        ask_kernel,
        out_shape=(
            jax.ShapeDtypeStruct((ranges, 128), BF16),
            jax.ShapeDtypeStruct(table.shape, BF16),
        ),
        in_specs=[vmem] * 2,
        out_specs=(vmem,) * 2,
        compiler_params=params,
        name="ask_rows",
    )(jnp.transpose(requests), table)
    asked = exchange(asks.reshape(chips, 2, 128), "chip")
    other_table = lax.ppermute(held, "core", swap)
    picked = pl.pallas_call(
        pick_kernel,
        out_shape=jax.ShapeDtypeStruct((ranges * cap, width), BF16),
        in_specs=[smem] + [vmem] * 3,
        out_specs=vmem,
        compiler_params=params,
        name="pick_rows",
    )(core, asked.reshape(ranges, 128), held, other_table)
    buffer = exchange(picked.reshape(chips, 2 * cap, width), "chip").reshape(ranges * cap, width)

    slab, moved = pl.pallas_call(
        functools.partial(step_kernel, float(length * ranges * tiles), share),
        out_shape=(
            jax.ShapeDtypeStruct((2, half, 128), BF16),
            jax.ShapeDtypeStruct((2 * length, 128), BF16),
        ),
        in_specs=[smem] + [vmem] * 13,
        out_specs=(vmem, vmem),
        scratch_shapes=[
            pltpu.VMEM((8, length), jnp.int32),
            pltpu.VMEM((16, 128), F32),
            pltpu.VMEM((HEADS, length, length), F32),
        ],
        compiler_params=params,
        name="window_step",
    )(
        core,
        features,
        buffer,
        jnp.transpose(ctx_slot[0]),
        labels,
        relay_slot,
        w_ctx,
        w_query,
        w_key,
        w_value,
        w_proj,
        w_logit,
        gain_attn.reshape(1, width),
        gain_out.reshape(1, width),
    )

    def total(parts):
        return lax.optimization_barrier(jnp.sum(parts.astype(F32), axis=0)).astype(BF16)

    other = lax.ppermute(slab[1], "core", swap)
    pair = (slab[0].astype(F32) + other.astype(F32)).astype(BF16)
    part = total(exchange(pair.reshape(tiles, quarter, 128), "dp"))
    piece = total(exchange(part.reshape(chips, pairs, 2, 128), "chip"))

    repeated = jnp.broadcast_to(piece[None], (chips, pairs, 2, 128))
    moved = moved.reshape(chips, moved_pairs, 2, 128)
    parts = exchange(jnp.concatenate([repeated, moved], axis=1), "chip")
    part, own_rows = lax.optimization_barrier((parts[:, :pairs], parts[:, pairs:]))
    part = jnp.broadcast_to(part.reshape(1, quarter, 128), (tiles, quarter, 128))
    own = exchange(part, "dp").reshape(half, 128)
    own_rows = own_rows.reshape(2 * length, 128)
    other = lax.ppermute(jnp.concatenate([own, own_rows], axis=0), "core", swap)

    square = jax.ShapeDtypeStruct((width, width), F32)
    line = jax.ShapeDtypeStruct((1, width), F32)
    outs = pl.pallas_call(
        functools.partial(unpack_kernel, share),
        out_shape=(
            jax.ShapeDtypeStruct((length, width), BF16),
            jax.ShapeDtypeStruct(w_ctx.shape, F32),
        )
        + (square,) * 5
        + (line, line, jax.ShapeDtypeStruct((1, 1), F32)),
        in_specs=[smem] + [vmem] * 3,
        out_specs=(vmem,) * 10,
        compiler_params=params,
        name="unpack",
    )(core, own, own_rows, other)
    return (
        outs[0][None],
        outs[9].reshape(()),
        outs[1],
        outs[2],
        outs[3],
        outs[4],
        outs[5],
        outs[6],
        outs[7].reshape(width),
        outs[8].reshape(width),
    )


def solution(mesh):
    ranges, tiles = mesh.devices.shape
    split = jax.sharding.Mesh(
        mesh.devices.reshape(ranges // 2, 2, tiles), ("chip", "core", "dp")
    )
    placed = (
        P("dp", RANGE, None),
        P("dp", RANGE, None),
        P("dp", RANGE, None, None),
        P("dp", RANGE, None),
        P("dp", RANGE),
        P("dp", RANGE),
        P(),
        P(),
        P(),
        P(),
        P(),
        P(),
        P(),
        P(),
    )
    return jax.shard_map(
        body,
        mesh=split,
        in_specs=placed,
        out_specs=(P("dp", RANGE, None), P(), P(), P(), P(), P(), P(), P(), P(), P()),
        check_vma=False,
    )
```
